128 devices in a mesh: section: 8 (over z_hi, x), tensor: 16 (over y, z_lo, core).
Axes of the slice: x: 4, y: 4, z: 4 (z_hi: 2, z_lo: 2; z = z_hi * 2 + z_lo), core: 2. Of those that a mesh axis runs over, the one named last changes fastest.
Arguments:
- local_codes: bfloat16 [8, 2, 512, 4096], P('section', None, 'tensor'), may hold values from -4 to 4
- local_scales: bfloat16 [8, 2, 512], P('section', None, 'tensor'), may hold values from 0.19921875 to 5
- parked_codes: bfloat16 [8, 2, 512, 4096], P('section', None, 'tensor'), may hold values from -4 to 4
- parked_scales: bfloat16 [8, 2, 512], P('section', None, 'tensor'), may hold values from 0.19921875 to 5
- keep_count: int32 [8], replicated, may hold values from 1 to 2, as said below
- roster: int32 [8], replicated, may hold values from 0 to 3, as said below
- norm_gain: float32 [8, 4096], P('section'), may hold values from 0.1 to 1.9
- w_gate: bfloat16 [8, 4096, 14336], P('section', None, 'tensor'), may hold values from -0.09375 to 0.09375
- w_up: bfloat16 [8, 4096, 14336], P('section', None, 'tensor'), may hold values from -0.09375 to 0.09375
- w_down: bfloat16 [8, 14336, 4096], P('section', 'tensor'), may hold values from -0.046875 to 0.046875
- pending: bfloat16 [8, 512, 4096], P('section', 'tensor'), may hold values from -6 to 6
Outputs:
- input_grad: bfloat16 [8, 512, 4096], P('section', 'tensor')
The draws below stay inside these ranges and needn't reach their ends.
Inputs may be any that keep to these rules, and one draw needn't show every extreme that they name: Sections s >= 4 keep every stash: keep_count[s] = 2. roster[s] < keep_count[s] + 2 for s < 4, and roster[s] < keep_count[s] for the other sections.
All inputs are finite; a program needn't handle non-finite values.
Results may differ from the reference program's by a relative error of at most 0.0058.
Values may be sent and summed in bfloat16 or wider, within the bound.
No kernel may reach another device: no remote copies, remote signals or barrier semaphores. Data moves between devices by JAX's collectives and lax.ppermute only.
A program may use at most 128 MiB of HBM per device.

```python
import math
import jax
import jax.numpy as jnp
from jax import lax

D = 4096
FF = 14336
ROWS = 512
LOCAL_SLOTS = 2
PARK_SLOTS = 2
N_SECTION = 8


def stash_plan(key):
    index = jnp.arange(N_SECTION)
    early = index < N_SECTION // 2
    keep = jax.random.randint(jax.random.fold_in(key, 11), (N_SECTION,), 1, LOCAL_SLOTS + 1)
    keep = jnp.where(early, keep, LOCAL_SLOTS)
    keep = keep.at[0].set(LOCAL_SLOTS)
    span = jnp.where(early, keep + PARK_SLOTS, keep)
    raw = jax.random.randint(jax.random.fold_in(key, 12), (N_SECTION,), 0, 1 << 20)
    slots = raw % span
    slots = slots.at[0].set(LOCAL_SLOTS + PARK_SLOTS - 1)
    last_early = N_SECTION // 2 - 1
    slots = slots.at[last_early].set(jnp.minimum(slots[last_early], keep[last_early] - 1))
    slots = slots.at[N_SECTION - 1].set(0)
    return (keep.astype(jnp.int32), slots.astype(jnp.int32))


def draw_keep_count(key, part):
    return stash_plan(key)[0]


def draw_roster(key, part):
    return stash_plan(key)[1]


def block_levels(key, dims, pieces, least, high):
    loudness = 1.0
    for axis_at, shards_of in pieces:
        steps = jax.random.uniform(jax.random.fold_in(jax.random.fold_in(key, 6), axis_at), (shards_of,), jnp.float32, least / len(pieces), high / len(pieces))
        loudness = loudness * jnp.repeat(jnp.exp(steps), dims[axis_at] // shards_of).reshape((-1,) + (1,) * (len(dims) - 1 - axis_at))
    return loudness


def bell_draw(rng, shape, spread, reach, pieces=(), held_as=jnp.bfloat16):
    entries = spread * jax.random.normal(rng, shape, jnp.float32)
    if pieces:
        entries = entries * block_levels(rng, shape, pieces, -0.22, 0.18)
    return jnp.clip(entries, -reach, reach).astype(held_as)


def setup_inputs(seed: int = 0) -> dict:
    key_list = jax.random.split(jax.random.key(seed), 12)
    local_codes = bell_draw(key_list[0], (N_SECTION, LOCAL_SLOTS, ROWS, D), 1.0, 4.0, ((0, 8), (2, 16)))
    local_scales = jnp.clip(jnp.exp(math.log(5.0) - 3.2227897 * jax.random.uniform(key_list[1], (N_SECTION, LOCAL_SLOTS, ROWS), jnp.float32) ** block_levels(key_list[1], (N_SECTION, LOCAL_SLOTS, ROWS), ((0, 8), (2, 16)), -0.2, 0.2)), 0.19921875, 5.0).astype(jnp.bfloat16)
    parked_codes = bell_draw(key_list[2], (N_SECTION, PARK_SLOTS, ROWS, D), 1.0, 4.0, ((0, 8), (2, 16)))
    parked_scales = jnp.clip(jnp.exp(math.log(5.0) - 3.2227897 * jax.random.uniform(key_list[3], (N_SECTION, PARK_SLOTS, ROWS), jnp.float32) ** block_levels(key_list[3], (N_SECTION, PARK_SLOTS, ROWS), ((0, 8), (2, 16)), -0.2, 0.2)), 0.19921875, 5.0).astype(jnp.bfloat16)
    keep_count = draw_keep_count(jax.random.fold_in(key_list[11], 71), 0)
    roster = draw_roster(jax.random.fold_in(key_list[11], 71), 0)
    norm_gain = jnp.clip(1.0 + 0.18 * jax.random.normal(key_list[6], (N_SECTION, D), jnp.float32), 0.1, 1.9)
    w_gate = bell_draw(key_list[7], (N_SECTION, D, FF), D ** -0.5, 0.09375, ((0, 8), (2, 16)))
    w_up = bell_draw(key_list[8], (N_SECTION, D, FF), D ** -0.5, 0.09375, ((0, 8), (2, 16)))
    w_down = bell_draw(key_list[9], (N_SECTION, FF, D), FF ** -0.5, 0.046875, ((0, 8), (1, 16)))
    pending = bell_draw(key_list[10], (N_SECTION, ROWS, D), 1.0, 6.0, ((0, 8), (1, 16)))
    return dict(local_codes=local_codes, local_scales=local_scales, parked_codes=parked_codes, parked_scales=parked_scales, keep_count=keep_count, roster=roster, norm_gain=norm_gain, w_gate=w_gate, w_up=w_up, w_down=w_down, pending=pending)


def reference(local_codes, local_scales, parked_codes, parked_scales, keep_count, roster, norm_gain, w_gate, w_up, w_down, pending):

    def one_section(s):
        slot = roster[s]
        keep = keep_count[s]
        mirror = N_SECTION - 1 - s
        local_slot = jnp.clip(slot, 0, LOCAL_SLOTS - 1).astype(jnp.int32)
        park_slot = jnp.clip(slot - keep, 0, PARK_SLOTS - 1).astype(jnp.int32)
        is_parked = slot >= keep
        codes = jnp.where(is_parked, parked_codes[mirror, park_slot], local_codes[s, local_slot])
        scales = jnp.where(is_parked, parked_scales[mirror, park_slot], local_scales[s, local_slot])
        x = codes.astype(jnp.float32) * scales.astype(jnp.float32)[:, None]
        inv_rms = lax.rsqrt(lax.optimization_barrier(jnp.mean(x * x, axis=-1, keepdims=True)) + 1e-05)
        unit = x * inv_rms
        gain = norm_gain[s].astype(jnp.float32)
        normed = (unit * gain).astype(jnp.bfloat16)
        gate = jnp.dot(normed, w_gate[s], preferred_element_type=jnp.float32)
        up = jnp.dot(normed, w_up[s], preferred_element_type=jnp.float32)
        cot = pending[(s + 1) % N_SECTION]
        dh = jnp.dot(cot, w_down[s].T, preferred_element_type=jnp.float32)
        sig = jax.nn.sigmoid(gate)
        dgate = (dh * up * sig * (1.0 + gate * (1.0 - sig))).astype(jnp.bfloat16)
        dup = (dh * gate * sig).astype(jnp.bfloat16)
        dn = jnp.dot(dgate, w_gate[s].T, preferred_element_type=jnp.float32) + jnp.dot(dup, w_up[s].T, preferred_element_type=jnp.float32)
        dg = dn * gain
        result = cot.astype(jnp.float32) + inv_rms * (dg - unit * lax.optimization_barrier(jnp.mean(dg * unit, axis=-1, keepdims=True)))
        return result.astype(jnp.bfloat16)
    return lax.map(one_section, jnp.arange(N_SECTION, dtype=jnp.int32))
```

```python
import functools

import jax
import jax.numpy as jnp
from jax import lax
from jax.experimental import pallas as pl
from jax.experimental.pallas import tpu as pltpu
from jax.sharding import PartitionSpec as P

bf16 = jnp.bfloat16
f32 = jnp.float32
VMEM = pl.BlockSpec(memory_space=pltpu.VMEM)
SMEM = pl.BlockSpec(memory_space=pltpu.SMEM)
MIB = 1024 * 1024


def like(*shape, dtype=bf16):
    return jax.ShapeDtypeStruct(shape, dtype)


def local_kernel(body, outs, *operands, limit=16, in_specs=None, scratch=(), flops=0, touched=0):
    return pl.pallas_call(
        body,
        out_shape=outs,
        in_specs=in_specs or [VMEM] * len(operands),
        out_specs=jax.tree.map(lambda _: VMEM, outs),
        scratch_shapes=scratch,
        compiler_params=pltpu.CompilerParams(vmem_limit_bytes=limit * MIB),
        cost_estimate=pl.CostEstimate(flops=flops, bytes_accessed=touched, transcendentals=0),
    )(*operands)


def over_tensor(shard, move):
    return lax.ppermute(shard, "tensor", [(i, move(i)) for i in range(lax.axis_size("tensor"))])


def other_core(i):
    return i ^ 1


def other_z(i):
    return i ^ 2


def along_y(i, sign=1):
    step = sign * (1 if i % 2 == 0 else -1)
    return (i // 4 + step) % 4 * 4 + i % 4


def back_y(i):
    return along_y(i, -1)


def join(*pieces):
    rows = [p.shape[0] for p in pieces]

    def body(*refs):
        out, at = refs[-1], 0
        for ref, n in zip(refs[:-1], rows):
            out[at : at + n] = ref[...]
            at += n

    return local_kernel(body, like(sum(rows), pieces[0].shape[1]), *pieces)


def norm_kernel(pick, codes, scales, parked, gain, normed, unit, inv):
    d = codes.shape[-1]

    def rows(which, scale):
        x = which.astype(f32) * scale.astype(f32)[:, :1]
        inv_rms = lax.rsqrt(jnp.mean(x * x, axis=-1, keepdims=True) + 1e-05)
        u = x * inv_rms
        unit[...] = u
        inv[...] = jnp.broadcast_to(inv_rms, inv.shape)
        normed[...] = (u * gain[...]).astype(bf16)

    @pl.when(pick[0] == 0)
    def _():
        rows(codes[0], scales[0])

    @pl.when(pick[0] == 1)
    def _():
        rows(codes[1], scales[1])

    @pl.when(pick[0] == 2)
    def _():
        rows(parked[:, :d], parked[:, d:])


def gather_normed(own):
    from_z = over_tensor(own, other_z)
    mine = join(own, from_z)
    chip = join(mine, over_tensor(mine, other_core))
    ahead = over_tensor(chip, along_y)
    behind = over_tensor(ahead, other_core)
    far = over_tensor(ahead[:64], along_y)
    far_other = over_tensor(far, other_core)
    return chip, ahead, behind, far, far_other


def gather_cot(own):
    other = over_tensor(own, other_core)
    ahead = over_tensor(join(own, other), along_y)
    far = over_tensor(ahead[:32], along_y)
    from_z = over_tensor(join(own, ahead, far), other_z)
    return own, other, ahead, far, from_z, over_tensor(join(ahead, far), other_core), over_tensor(from_z, other_core)


def dh_kernel(own, other, ahead, far, from_z, swapped, swapped_z, w_down, dh, rows):
    at = 0

    def put(ref, k):
        nonlocal at
        rows[at : at + 32] = ref[32 * k : 32 * k + 32]
        at += 32

    for block in (own, (ahead, 0), (ahead, 1), far):
        ref, k = block if isinstance(block, tuple) else (block, 0)
        put(ref, k)
        put(from_z, at // 64)
    for ref, k in ((other, 0), (swapped, 0), (swapped, 1), (swapped, 2)):
        put(ref, k)
        put(swapped_z, (at - 256) // 64)
    dh[...] = lax.dot_general(rows[...], w_down[...], (((1,), (1,)), ((), ())), preferred_element_type=f32)


def hidden_kernel(blocks, *refs):
    pieces, (dh, w_gate, w_up, dgate, dup, rows) = refs[:-6], refs[-6:]
    for (piece, start, count, at, dh_at) in blocks:
        rows[at : at + count] = pieces[piece][start : start + count]
    gate = jnp.dot(rows[...], w_gate[...], preferred_element_type=f32)
    up = jnp.dot(rows[...], w_up[...], preferred_element_type=f32)
    for (piece, start, count, at, dh_at) in blocks:
        g, u, d = gate[at : at + count], up[at : at + count], dh[dh_at : dh_at + count]
        sig = jax.nn.sigmoid(g)
        dgate[at : at + count] = (d * u * sig * (1.0 + g * (1.0 - sig))).astype(bf16)
        dup[at : at + count] = (d * g * sig).astype(bf16)


def back_kernel(half, near_g, near_u, far_g, far_u, w_gate, w_up, keep, send, g_rows, u_rows):
    for rows, near, far in ((g_rows, near_g, far_g), (u_rows, near_u, far_u)):
        rows[0:192] = near[0:192]
        rows[192:256] = far[0:64]
        rows[256:448] = near[192:384]
        rows[448:512] = far[64:128]
    n = keep.shape[1]
    cols = slice(half * n, half * n + n)
    transposed = (((1,), (1,)), ((), ()))
    dn = lax.dot_general(g_rows[...], w_gate[cols, :], transposed, preferred_element_type=f32) + lax.dot_general(
        u_rows[...], w_up[cols, :], transposed, preferred_element_type=f32
    )
    keep[...] = dn[:256].astype(bf16)
    send[...] = dn[256:].astype(bf16)


def add(*pieces, spans, rows):
    def body(*refs):
        for at, count, terms in spans:
            total = None
            for piece, start in terms:
                term = refs[piece][start : start + count].astype(f32)
                total = term if total is None else total + term
            refs[-1][at : at + count] = total.astype(bf16)

    return local_kernel(body, like(rows, pieces[0].shape[1]), *pieces)


def scatter_y_first(keep, send):
    got = over_tensor(send, other_core)
    far = add(keep, got, spans=[(0, 64, ((0, 192), (1, 192)))], rows=64)
    far_got = over_tensor(far, back_y)
    ahead = add(keep, got, far_got, spans=[(0, 64, ((0, 64), (1, 64), (2, 0))), (64, 64, ((0, 128), (1, 128)))], rows=128)
    home = over_tensor(ahead, back_y)
    home_other = over_tensor(home[64:], other_core)
    total = add(keep, got, home, home_other, spans=[(0, 64, ((0, 0), (1, 0), (2, 0), (3, 0)))], rows=64)
    return total, over_tensor(total[32:], other_z)


def scatter_z_first(keep, send):
    got = over_tensor(send, other_core)
    away = add(keep, got, spans=[(32 * b, 32, ((0, 64 * b + 32), (1, 64 * b + 32))) for b in range(4)], rows=128)
    from_z = over_tensor(away, other_z)
    held = add(keep, got, from_z, spans=[(32 * b, 32, ((0, 64 * b), (1, 64 * b), (2, 32 * b))) for b in range(4)], rows=128)
    far_got = over_tensor(held[96:], back_y)
    ahead = add(held, far_got, spans=[(0, 32, ((0, 32), (1, 0))), (32, 32, ((0, 64),))], rows=64)
    home = over_tensor(ahead, back_y)
    return held, home, over_tensor(home[32:], other_core)


def final_kernel(total, from_z, held, home, home_other, cot, unit, inv, gain, out):
    half = total.shape[1]
    dn_a = total[:32].astype(f32) + from_z[...].astype(f32)
    dn_b = held[:32].astype(f32) + home[:32].astype(f32) + home_other[...].astype(f32)
    g_a, g_b = dn_a * gain[:, :half], dn_b * gain[:, half:]
    u_a, u_b = unit[:, :half], unit[:, half:]
    mean = (
        jnp.sum(g_a * u_a, axis=-1, keepdims=True) + jnp.sum(g_b * u_b, axis=-1, keepdims=True)
    ) / (2 * half)
    scale = inv[:, :1]
    out[:, :half] = (cot[:, :half].astype(f32) + scale * (g_a - u_a * mean)).astype(bf16)
    out[:, half:] = (cot[:, half:].astype(f32) + scale * (g_b - u_b * mean)).astype(bf16)


def on_device(
    local_codes,
    local_scales,
    parked_codes,
    parked_scales,
    keep_count,
    roster,
    norm_gain,
    w_gate,
    w_up,
    w_down,
    pending,
):
    sections = lax.axis_size("section")
    mine = lax.axis_index("section")
    _, _, shard, d = local_codes.shape
    hidden = w_gate.shape[2]
    rows = 16 * shard

    cot = lax.ppermute(pending[0], "section", [((i + 1) % sections, i) for i in range(sections)])
    mirror = sections - 1 - mine
    asked = jnp.clip(roster[mirror] - keep_count[mirror], 0, 1)
    payload = jnp.concatenate(
        [
            lax.dynamic_index_in_dim(parked_codes[0], asked, 0, keepdims=False),
            jnp.broadcast_to(lax.dynamic_index_in_dim(parked_scales[0], asked, 0, keepdims=False)[:, None], (shard, 128)),
        ],
        axis=1,
    )
    fetched = lax.ppermute(payload, "section", [(sections - 1 - i, i) for i in range(sections // 2)])
    is_parked = roster[mine] >= keep_count[mine]
    pick = jnp.where(is_parked, 2, jnp.clip(roster[mine], 0, 1)).astype(jnp.int32)[None]

    gain = norm_gain
    normed, unit, inv = local_kernel(
        norm_kernel,
        (like(shard, d), like(shard, d, dtype=f32), like(shard, 128, dtype=f32)),
        pick,
        local_codes[0],
        jnp.broadcast_to(local_scales[0][:, :, None], (2, shard, 128)),
        fetched,
        gain,
        in_specs=[SMEM] + [VMEM] * 4,
    )

    cots = gather_cot(cot)
    chip, ahead, behind, far, far_other = gather_normed(normed)

    dh = local_kernel(
        dh_kernel,
        like(rows, hidden, dtype=f32),
        *cots,
        w_down[0],
        limit=26,
        scratch=[pltpu.VMEM((rows, d), bf16)],
        flops=2 * rows * d * hidden,
    )
    near_blocks = ((0, 0, 64, 0, 0), (1, 0, 128, 64, 64), (0, 64, 64, 192, 256), (2, 0, 128, 256, 320))
    far_blocks = ((0, 0, 64, 0, 192), (1, 0, 64, 64, 448))
    near_g, near_u = local_kernel(
        functools.partial(hidden_kernel, near_blocks),
        (like(384, hidden), like(384, hidden)),
        chip,
        ahead,
        behind,
        dh,
        w_gate[0],
        w_up[0],
        limit=34,
        scratch=[pltpu.VMEM((384, d), bf16)],
        flops=4 * 384 * d * hidden,
    )
    far_g, far_u = local_kernel(
        functools.partial(hidden_kernel, far_blocks),
        (like(128, hidden), like(128, hidden)),
        far,
        far_other,
        dh,
        w_gate[0],
        w_up[0],
        limit=34,
        scratch=[pltpu.VMEM((128, d), bf16)],
        flops=4 * 128 * d * hidden,
    )

    def back(half):
        return local_kernel(
            functools.partial(back_kernel, half),
            (like(256, d // 2), like(256, d // 2)),
            near_g,
            near_u,
            far_g,
            far_u,
            w_gate[0],
            w_up[0],
            limit=34,
            scratch=[pltpu.VMEM((rows, hidden), bf16)] * 2,
            flops=2 * rows * d * hidden,
        )

    held, home, home_other = scatter_z_first(*back(1))
    total, from_z = scatter_y_first(*back(0))
    return local_kernel(
        final_kernel, like(shard, d), total, from_z, held, home, home_other, cot, unit, inv, gain
    )[None]


def solution(mesh):
    placed = (
        P("section", None, "tensor", None),
        P("section", None, "tensor"),
        P("section", None, "tensor", None),
        P("section", None, "tensor"),
        P(),
        P(),
        P("section", None),
        P("section", None, "tensor"),
        P("section", None, "tensor"),
        P("section", "tensor", None),
        P("section", "tensor", None),
    )
    return jax.shard_map(
        on_device,
        mesh=mesh,
        in_specs=placed,
        out_specs=P("section", "tensor", None),
        check_vma=False,
    )
```

```python
import functools

import jax
import jax.numpy as jnp
from jax import lax
from jax.experimental import pallas as pl
from jax.experimental.pallas import tpu as pltpu
from jax.sharding import PartitionSpec as P

bf16 = jnp.bfloat16
f32 = jnp.float32
VMEM = pl.BlockSpec(memory_space=pltpu.VMEM)
MIB = 1024 * 1024
LONG = 10**11
Y_FIRST = 1792
EXTRA = 512
HIDDEN_LIMIT = 14
BACK_LIMIT = 16


def like(*shape, dtype=bf16):
    return jax.ShapeDtypeStruct(shape, dtype)


def local_kernel(name, body, outs, *operands, after=(), hbm=False, limit=12, scratch=(), flops=1):
    n_in, n_after = len(operands), len(after)
    anywhere = pl.BlockSpec(memory_space=pl.ANY)
    if hbm:
        operands = tuple(pltpu.with_memory_space_constraint(o, pltpu.HBM) for o in operands)

    def run(*refs):
        body(*refs[:n_in], *refs[n_in + n_after :])

    return pl.pallas_call(
        run,
        out_shape=outs,
        in_specs=[anywhere if hbm else VMEM] * n_in + [anywhere] * n_after,
        out_specs=jax.tree.map(lambda _: VMEM, outs),
        scratch_shapes=scratch,
        compiler_params=pltpu.CompilerParams(vmem_limit_bytes=limit * MIB),
        cost_estimate=pl.CostEstimate(flops=flops, bytes_accessed=1, transcendentals=0),
        name=name,
    )(*operands, *after)


def over_tensor(name, shard, move):
    with jax.named_scope(name):
        return lax.ppermute(shard, "tensor", [(i, move(i)) for i in range(lax.axis_size("tensor"))])


def other_core(i):
    return i ^ 1


def other_z(i):
    return i ^ 2


def along_y(i, sign=1):
    step = sign * (1 if i % 2 == 0 else -1)
    return (i // 4 + step) % 4 * 4 + i % 4


def back_y(i):
    return along_y(i, -1)


def across_y(i):
    return (i + 8) % 16


def join(name, *pieces, after=(), flops=1):
    pieces = [p if isinstance(p, tuple) else (p, 0, p.shape[0]) for p in pieces]

    def body(*refs):
        out, at = refs[-1], 0
        for ref, (_, start, n) in zip(refs[:-1], pieces):
            out[at : at + n] = ref[start : start + n]
            at += n

    rows = sum(n for _, _, n in pieces)
    return local_kernel(name, body, like(rows, pieces[0][0].shape[1]), *[p for p, _, _ in pieces], after=after, flops=flops)


def prepare_kernel(keep_hbm, roster_hbm, parked, parked_scale, local, local_scale, gain, pending,
                   payload, own, gain_copy, cot, codes, scales, keep, roster, sems):
    mine = lax.axis_index("section")
    mirror = lax.axis_size("section") - 1 - mine
    d = gain.shape[1]
    copies = [
        pltpu.make_async_copy(source, target, sems.at[k])
        for k, (source, target) in enumerate(
            (
                (parked, codes.at[0]),
                (parked_scale, scales.at[0]),
                (local, codes.at[1]),
                (local_scale, scales.at[1]),
                (gain, gain_copy),
                (pending, cot),
                (keep_hbm, keep),
                (roster_hbm, roster),
            )
        )
    ]
    for copy in copies:
        copy.start()

    def put(out, which, slot):
        rows = codes.shape[2]
        eye = lax.broadcasted_iota(jnp.int32, (rows, rows), 0) == lax.broadcasted_iota(jnp.int32, (rows, rows), 1)

        def choose(k):
            out[:, :d] = codes[which, k]
            row = jnp.broadcast_to(scales[which, k : k + 1, :].astype(f32), (rows, rows))
            column = jnp.sum(jnp.where(eye, row, 0.0), axis=1, keepdims=True)
            out[:, d : d + EXTRA] = jnp.broadcast_to(column, (rows, EXTRA)).astype(bf16)

        pl.when(slot <= 0)(lambda: choose(0))
        pl.when(slot > 0)(lambda: choose(1))

    for k in (6, 7, 0, 1):
        copies[k].wait()
    put(payload, 0, roster[mirror] - keep[mirror])
    copies[2].wait()
    copies[3].wait()
    put(own, 1, roster[mine])
    is_parked = (roster[mine] >= keep[mine]).astype(f32)
    own[:, d + EXTRA :] = jnp.full((own.shape[0], 128), is_parked, f32).astype(bf16)
    copies[4].wait()
    copies[5].wait()


def norm_kernel(own, parked, gain, normed, unit, inv):
    d = gain.shape[1]
    is_parked = own[:, d + EXTRA : d + EXTRA + 1] > 0
    codes = jnp.where(is_parked, parked[:, :d], own[:, :d])
    scale = jnp.where(is_parked, parked[:, d : d + 1], own[:, d : d + 1])
    x = codes.astype(f32) * scale.astype(f32)
    inv_rms = lax.rsqrt(jnp.mean(x * x, axis=-1, keepdims=True) + 1e-05)
    u = x * inv_rms
    unit[...] = u
    inv[...] = jnp.broadcast_to(inv_rms, inv.shape)
    normed[...] = (u * gain[...]).astype(bf16)


def hidden_kernel(cot_blocks, normed_blocks, n_cot, n_normed, *refs):
    cots, normeds = refs[:n_cot], refs[n_cot : n_cot + n_normed]
    w_gate, w_up, w_down, dgate, dup, rows, dh = refs[n_cot + n_normed :]

    def fill(pieces, blocks):
        at = 0
        for piece, start, count in blocks:
            rows[at : at + count] = pieces[piece][start : start + count]
            at += count

    fill(cots, cot_blocks)
    dh[...] = lax.dot_general(rows[...], w_down[...], (((1,), (1,)), ((), ())), preferred_element_type=f32)
    fill(normeds, normed_blocks)
    gate = jnp.dot(rows[...], w_gate[...], preferred_element_type=f32)
    up = jnp.dot(rows[...], w_up[...], preferred_element_type=f32)
    d = dh[...]
    sig = jax.nn.sigmoid(gate)
    dgate[...] = (d * up * sig * (1.0 + gate * (1.0 - sig))).astype(bf16)
    dup[...] = (d * gate * sig).astype(bf16)


def hidden(name, cots, cot_blocks, normeds, normed_blocks, weights, after=()):
    n_rows = sum(count for _, _, count in cot_blocks)
    d, units = weights[0].shape
    return local_kernel(
        name,
        functools.partial(hidden_kernel, cot_blocks, normed_blocks, len(cots), len(normeds)),
        (like(n_rows, units), like(n_rows, units)),
        *cots,
        *normeds,
        *weights,
        after=after,
        scratch=[pltpu.VMEM((n_rows, d), bf16), pltpu.VMEM((n_rows, units), f32)],
        flops=LONG,
        limit=HIDDEN_LIMIT,
    )


def back_kernel(start, g0, u0, g1, u1, g2, u2, w_gate, w_up, keep, send, g_rows, u_rows):
    for rows, home, side, far in ((g_rows, g0, g1, g2), (u_rows, u0, u1, u2)):
        rows[0:64] = home[0:64]
        rows[64:192] = side[0:128]
        rows[192:256] = far[0:64]
        rows[256:320] = home[64:128]
        rows[320:448] = side[128:256]
        rows[448:512] = far[64:128]
    n = keep.shape[1]
    cols = slice(start, start + n)
    transposed = (((1,), (1,)), ((), ()))
    dn = lax.dot_general(g_rows[...], w_gate[cols, :], transposed, preferred_element_type=f32) + lax.dot_general(
        u_rows[...], w_up[cols, :], transposed, preferred_element_type=f32
    )
    keep[...] = dn[:256].astype(bf16)
    send[...] = dn[256:].astype(bf16)


def back(name, start, n, grads, w_gate, w_up, after=()):
    units = w_gate.shape[1]
    return local_kernel(
        name,
        functools.partial(back_kernel, start),
        (like(256, n), like(256, n)),
        *grads,
        w_gate,
        w_up,
        after=after,
        scratch=[pltpu.VMEM((512, units), bf16)] * 2,
        flops=LONG,
        limit=BACK_LIMIT,
    )


def add(name, outs, *columns, after=()):
    widths = [pieces[0].shape[1] for pieces in columns]
    n_in = sum(len(pieces) for pieces in columns)

    def body(*refs):
        for out, spans in zip(refs[n_in:], outs):
            left, at_piece = 0, 0
            for pieces, width in zip(columns, widths):
                at = 0
                for count, terms in spans:
                    total = None
                    for piece, start in terms:
                        term = refs[at_piece + piece][start : start + count].astype(f32)
                        total = term if total is None else total + term
                    out[at : at + count, left : left + width] = total.astype(bf16)
                    at += count
                left += width
                at_piece += len(pieces)

    shapes = tuple(like(sum(count for count, _ in spans), sum(widths)) for spans in outs)
    results = local_kernel(name, body, shapes, *[p for pieces in columns for p in pieces], after=after)
    return results if len(outs) > 1 else results[0]


def final_kernel(held, far_b, home_b, other_b, total, total_z, cot, unit, inv, gain, out):
    split = total.shape[1]
    dn_a = total[...].astype(f32) + total_z[...].astype(f32)
    dn_b = held[...].astype(f32) + far_b[...].astype(f32) + home_b[:32].astype(f32) + other_b[...].astype(f32)
    g_a, g_b = dn_a * gain[:, :split], dn_b * gain[:, split:]
    u_a, u_b = unit[:, :split], unit[:, split:]
    mean = (
        jnp.sum(g_a * u_a, axis=-1, keepdims=True) + jnp.sum(g_b * u_b, axis=-1, keepdims=True)
    ) / unit.shape[1]
    scale = inv[:, :1]
    out[:, :split] = (cot[:, :split].astype(f32) + scale * (g_a - u_a * mean)).astype(bf16)
    out[:, split:] = (cot[:, split:].astype(f32) + scale * (g_b - u_b * mean)).astype(bf16)


def on_device(
    local_codes,
    local_scales,
    parked_codes,
    parked_scales,
    keep_count,
    roster,
    norm_gain,
    w_gate,
    w_up,
    w_down,
    pending,
):
    sections = lax.axis_size("section")
    _, _, shard, d = local_codes.shape
    stash_pairs = [(sections - 1 - i, i) for i in range(sections // 2)]
    shift_pairs = [((i + 1) % sections, i) for i in range(sections)]

    payload, own_stash, gain, cot_source = local_kernel(
        "prepare",
        prepare_kernel,
        (like(shard, d + EXTRA), like(shard, d + EXTRA + 128), like(1, d, dtype=f32), like(shard, d)),
        keep_count,
        roster,
        parked_codes[0],
        parked_scales[0],
        local_codes[0],
        local_scales[0],
        norm_gain,
        pending[0],
        hbm=True,
        scratch=[
            pltpu.VMEM((2, 2, shard, d), bf16),
            pltpu.VMEM((2, 2, shard), bf16),
            pltpu.SMEM(keep_count.shape, jnp.int32),
            pltpu.SMEM(roster.shape, jnp.int32),
            pltpu.SemaphoreType.DMA((8,)),
        ],
    )
    with jax.named_scope("fetched"):
        fetched = lax.ppermute(payload, "section", stash_pairs)
    with jax.named_scope("shift"):
        cot = lax.ppermute(cot_source, "section", shift_pairs)
    w_gate, w_up, w_down = w_gate[0], w_up[0], w_down[0]
    weights = w_gate, w_up, w_down
    cot = join("cot", cot, after=(own_stash,))
    cot_z = over_tensor("cot_z", cot, other_z)
    cot_core = over_tensor("cot_core", cot, other_core)
    cot_chip = join("cot_chip", cot, cot_core)
    cot_ahead = over_tensor("cot_ahead", cot_chip, along_y)

    normed, unit, inv = local_kernel(
        "norm",
        norm_kernel,
        (like(shard, d), like(shard, d, dtype=f32), like(shard, 128, dtype=f32)),
        own_stash,
        fetched,
        gain,
        after=(cot_chip,),
        flops=LONG,
    )
    normed_z = over_tensor("normed_z", normed, other_z)
    normed_core = over_tensor("normed_core", normed, other_core)
    cot_part = join("cot_part", (cot_ahead, 0, 32), after=(normed, cot_z))
    cot_far = over_tensor("cot_far", cot_part, along_y)
    cot_ahead_z = over_tensor("cot_ahead_z", cot_ahead, other_z)
    cot_behind = over_tensor("cot_behind", cot_ahead, other_core)
    cot_z_core = over_tensor("cot_z_core", cot_z, other_core)

    ahead = over_tensor("ahead", join("chip", normed, normed_core), along_y)
    normed_z_core = over_tensor("normed_z_core", join("normed_z_copy", normed_z, after=(cot_part,)), other_core)
    chip_z = join("chip_z", normed_z, normed_z_core)
    ahead_z = over_tensor("ahead_z", chip_z, along_y)
    cot_far_z = over_tensor("cot_far_z", cot_far, other_z)
    cot_far_core = over_tensor("cot_far_core", cot_far, other_core)
    g0, u0 = hidden(
        "hidden_home",
        (cot, cot_z, cot_core, cot_z_core),
        tuple((k, 0, 32) for k in range(4)),
        (normed, normed_z, normed_core, normed_z_core),
        tuple((k, 0, 32) for k in range(4)),
        weights,
        after=(cot_ahead_z, cot_far),
    )
    cot_behind_z = over_tensor("cot_behind_z", cot_ahead_z, other_core)
    far = over_tensor("far", join("part", (ahead, 0, 32), (ahead_z, 0, 32), after=(g0,)), along_y)
    behind = over_tensor("behind", join("ahead_copy", ahead, after=(g0,)), other_core)
    behind_z = over_tensor("behind_z", join("ahead_z_copy", ahead_z, after=(g0,)), other_core)
    sides = tuple((k + j, 32 * h, 32) for k in (0, 2) for h in range(2) for j in range(2))
    g1, u1 = hidden(
        "hidden_sides",
        (cot_ahead, cot_ahead_z, cot_behind, cot_behind_z),
        sides,
        (ahead, ahead_z, behind, behind_z),
        sides,
        weights,
    )
    cot_far_z_core = over_tensor("cot_far_z_core", join("cot_far_z_copy", cot_far_z, after=(g1,)), other_core)
    far_core = over_tensor("far_core", join("far_copy", far, after=(g1,)), other_core)
    g2, u2 = hidden(
        "hidden_far",
        (cot_far, cot_far_z, cot_far_core, cot_far_z_core),
        tuple((k, 0, 32) for k in range(4)),
        (far, far_core),
        ((0, 0, 64), (1, 0, 64)),
        weights,
    )
    grads = (g0, u0, g1, u1, g2, u2)

    keep_a, send_a = back("back_a", 0, Y_FIRST, grads, w_gate, w_up)
    got_a = over_tensor("got_a", send_a, other_core)
    keep_b, send_b = back("back_b", Y_FIRST, d - Y_FIRST, grads, w_gate, w_up, after=(keep_a,))
    got_b = over_tensor("got_b", send_b, other_core)
    both = keep_a, got_a
    to_far = add("to_far", [[(64, ((0, 192), (1, 192)))]], both, after=(keep_b,))
    from_far = over_tensor("from_far", to_far, back_y)
    away = add("away", [[(32, ((0, 64 * k + 32), (1, 64 * k + 32))) for k in range(4)]], (keep_b, got_b), after=(to_far,))
    from_z = over_tensor("from_z", away, other_z)
    near, side = add("near_side", [[(64, ((0, 0), (1, 0)))], [(128, ((0, 64), (1, 64)))]], both, after=(away,))
    to_home = add("to_home", [[(64, ((0, 0), (1, 0))), (64, ((0, 64),))]], (side, from_far))
    home = over_tensor("home", to_home, back_y)
    held, held_side, held_far = add(
        "held",
        [
            [(32, ((0, 64 * k), (1, 64 * k), (2, 32 * k))) for k in ks]
            for ks in ((0,), (1, 2), (3,))
        ],
        (keep_b, got_b, from_z),
    )
    home_core = tuple(
        over_tensor(name, join(name + "_part", (home, at, 32), after=(held,)), other_core)
        for name, at in (("home_core", 64), ("home_core_z", 96))
    )
    total, total_away = add(
        "total", [[(32, ((0, at), (1, at), (2 + at // 32, 0)))] for at in (0, 32)], (near, home, *home_core)
    )
    total_z = over_tensor("total_z", total_away, other_z)
    home_b = over_tensor("home_b", held_side, back_y)
    far_b = over_tensor("far_b", held_far, across_y)
    home_b_core = over_tensor("home_b_core", join("home_b_part", (home_b, 32, 32), after=(total, far_b)), other_core)
    return local_kernel(
        "final", final_kernel, like(shard, d), held, far_b, home_b, home_b_core, total, total_z, cot, unit, inv, gain
    )[None]


def solution(mesh):
    placed = (
        P("section", None, "tensor", None),
        P("section", None, "tensor"),
        P("section", None, "tensor", None),
        P("section", None, "tensor"),
        P(),
        P(),
        P("section", None),
        P("section", None, "tensor"),
        P("section", None, "tensor"),
        P("section", "tensor", None),
        P("section", "tensor", None),
    )
    return jax.shard_map(
        on_device,
        mesh=mesh,
        in_specs=placed,
        out_specs=P("section", "tensor", None),
        check_vma=False,
    )
```

```python
import functools

import jax
import jax.numpy as jnp
from jax import lax
from jax.experimental import pallas as pl
from jax.experimental.pallas import tpu as pltpu
from jax.sharding import PartitionSpec as P

bf16 = jnp.bfloat16
f32 = jnp.float32
VMEM = pl.BlockSpec(memory_space=pltpu.VMEM)
MIB = 1024 * 1024
LONG = 10**11
Y_FIRST = 2688
EXTRA = 512
SHORT = 10**9
PARTS = (0, 48), (48, 16)
HIDDEN_LIMIT = 10
BACK_LIMIT = 10


def like(*shape, dtype=bf16):
    return jax.ShapeDtypeStruct(shape, dtype)


def local_kernel(name, body, outs, *operands, after=(), hbm=False, limit=12, scratch=(), flops=1):
    n_in, n_after = len(operands), len(after)
    anywhere = pl.BlockSpec(memory_space=pl.ANY)
    if hbm:
        operands = tuple(pltpu.with_memory_space_constraint(o, pltpu.HBM) for o in operands)

    def run(*refs):
        body(*refs[:n_in], *refs[n_in + n_after :])

    return pl.pallas_call(
        run,
        out_shape=outs,
        in_specs=[anywhere if hbm else VMEM] * n_in + [anywhere] * n_after,
        out_specs=jax.tree.map(lambda _: VMEM, outs),
        scratch_shapes=scratch,
        compiler_params=pltpu.CompilerParams(vmem_limit_bytes=limit * MIB),
        cost_estimate=pl.CostEstimate(flops=flops, bytes_accessed=1, transcendentals=0),
        name=name,
    )(*operands, *after)


def over_tensor(name, shard, move):
    with jax.named_scope(name):
        return lax.ppermute(shard, "tensor", [(i, move(i)) for i in range(lax.axis_size("tensor"))])


def other_core(i):
    return i ^ 1


def other_z(i):
    return i ^ 2


def along_y(i, sign=1):
    step = sign * (1 if i % 2 == 0 else -1)
    return (i // 4 + step) % 4 * 4 + i % 4


def back_y(i):
    return along_y(i, -1)


def across_y(i):
    return (i + 8) % 16


def join(name, *pieces, after=(), columns=None, flops=1):
    pieces = [p if isinstance(p, tuple) else (p, 0, p.shape[0]) for p in pieces]
    columns = columns or pieces[0][0].shape[1]

    def body(*refs):
        out, at = refs[-1], 0
        for ref, (_, start, n) in zip(refs[:-1], pieces):
            have = min(columns, ref.shape[1])
            out[at : at + n, :have] = ref[start : start + n, :have]
            if have < columns:
                out[at : at + n, have:] = ref[start : start + n, : columns - have]
            at += n

    rows = sum(n for _, _, n in pieces)
    return local_kernel(name, body, like(rows, columns), *[p for p, _, _ in pieces], after=after, flops=flops)


def prepare_kernel(keep_hbm, roster_hbm, parked, parked_scale, local, local_scale, gain, pending,
                   payload, own, gain_copy, cot, codes, scales, keep, roster, sems):
    mine = lax.axis_index("section")
    mirror = lax.axis_size("section") - 1 - mine
    d = gain.shape[1]
    copies = [
        pltpu.make_async_copy(source, target, sems.at[k])
        for k, (source, target) in enumerate(
            (
                (parked, codes.at[0]),
                (parked_scale, scales.at[0]),
                (local, codes.at[1]),
                (local_scale, scales.at[1]),
                (gain, gain_copy),
                (pending, cot),
                (keep_hbm, keep),
                (roster_hbm, roster),
            )
        )
    ]
    for copy in copies:
        copy.start()

    def put(out, which, slot):
        rows = codes.shape[2]
        eye = lax.broadcasted_iota(jnp.int32, (rows, rows), 0) == lax.broadcasted_iota(jnp.int32, (rows, rows), 1)

        def choose(k):
            out[:, :d] = codes[which, k]
            row = jnp.broadcast_to(scales[which, k : k + 1, :].astype(f32), (rows, rows))
            column = jnp.sum(jnp.where(eye, row, 0.0), axis=1, keepdims=True)
            out[:, d : d + EXTRA] = jnp.broadcast_to(column, (rows, EXTRA)).astype(bf16)

        pl.when(slot <= 0)(lambda: choose(0))
        pl.when(slot > 0)(lambda: choose(1))

    for k in (6, 7, 0, 1):
        copies[k].wait()
    put(payload, 0, roster[mirror] - keep[mirror])
    copies[2].wait()
    copies[3].wait()
    put(own, 1, roster[mine])
    is_parked = (roster[mine] >= keep[mine]).astype(f32)
    own[:, d + EXTRA :] = jnp.full((own.shape[0], 128), is_parked, f32).astype(bf16)
    copies[4].wait()
    copies[5].wait()


def norm_kernel(own, parked, gain, normed, unit, inv):
    d = gain.shape[1]
    is_parked = own[:, d + EXTRA : d + EXTRA + 1] > 0
    codes = jnp.where(is_parked, parked[:, :d], own[:, :d])
    scale = jnp.where(is_parked, parked[:, d : d + 1], own[:, d : d + 1])
    x = codes.astype(f32) * scale.astype(f32)
    inv_rms = lax.rsqrt(jnp.mean(x * x, axis=-1, keepdims=True) + 1e-05)
    u = x * inv_rms
    unit[...] = u
    inv[...] = jnp.broadcast_to(inv_rms, inv.shape)
    normed[...] = (u * gain[...]).astype(bf16)


def hidden_kernel(cot_blocks, normed_blocks, n_cot, n_normed, *refs):
    cots, normeds = refs[:n_cot], refs[n_cot : n_cot + n_normed]
    w_gate, w_up, w_down, dgate, dup, rows, dh = refs[n_cot + n_normed :]

    def fill(pieces, blocks):
        at = 0
        for piece, start, count in blocks:
            rows[at : at + count] = pieces[piece][start : start + count, : rows.shape[1]]
            at += count

    fill(cots, cot_blocks)
    dh[...] = lax.dot_general(rows[...], w_down[...], (((1,), (1,)), ((), ())), preferred_element_type=f32)
    fill(normeds, normed_blocks)
    gate = jnp.dot(rows[...], w_gate[...], preferred_element_type=f32)
    up = jnp.dot(rows[...], w_up[...], preferred_element_type=f32)
    d = dh[...]
    sig = jax.nn.sigmoid(gate)
    dgate[...] = (d * up * sig * (1.0 + gate * (1.0 - sig))).astype(bf16)
    dup[...] = (d * gate * sig).astype(bf16)


def hidden(name, cots, cot_blocks, normeds, normed_blocks, weights, after=(), flops=1):
    n_rows = sum(count for _, _, count in cot_blocks)
    d, units = weights[0].shape
    return local_kernel(
        name,
        functools.partial(hidden_kernel, cot_blocks, normed_blocks, len(cots), len(normeds)),
        (like(n_rows, units), like(n_rows, units)),
        *cots,
        *normeds,
        *weights,
        after=after,
        scratch=[pltpu.VMEM((n_rows, d), bf16), pltpu.VMEM((n_rows, units), f32)],
        flops=flops,
        limit=HIDDEN_LIMIT,
    )


def back(name, start, n, outs, grads, w_gate, w_up, after=(), flops=1):
    def body(g, u, w_gate, w_up, *results):
        cols = slice(start, start + n)
        transposed = (((1,), (1,)), ((), ()))
        dn = lax.dot_general(g[...], w_gate[cols, :], transposed, preferred_element_type=f32) + lax.dot_general(
            u[...], w_up[cols, :], transposed, preferred_element_type=f32
        )
        for result, spans in zip(results, outs):
            at = 0
            for first, count in spans:
                result[at : at + count] = dn[first : first + count].astype(bf16)
                at += count

    shapes = tuple(like(sum(count for _, count in spans), n) for spans in outs)
    return local_kernel(name, body, shapes, *grads, w_gate, w_up, after=after, flops=flops, limit=BACK_LIMIT)


def add(name, width, outs, *pieces, after=()):
    pieces = [p if isinstance(p, tuple) else (p, 0) for p in pieces]

    def body(*refs):
        for out, spans in zip(refs[len(pieces) :], outs):
            at = 0
            for count, terms in spans:
                total = None
                for piece, start in terms:
                    left = pieces[piece][1]
                    term = refs[piece][start : start + count, left : left + width].astype(f32)
                    total = term if total is None else total + term
                out[at : at + count] = total.astype(out.dtype)
                at += count

    shapes = tuple(like(sum(count for count, _ in spans), width) for spans in outs)
    results = local_kernel(name, body, shapes, *[p for p, _ in pieces], after=after)
    return results if len(outs) > 1 else results[0]


def final_kernel(held, home_far, home_b, other_b, total, total_z, cot, unit, inv, gain, out):
    split = total.shape[1]
    dn_a = total[...].astype(f32) + total_z[...].astype(f32)
    dn_b = held[...].astype(f32) + home_far[...].astype(f32) + home_b[:32].astype(f32) + other_b[...].astype(f32)
    g_a, g_b = dn_a * gain[:, :split], dn_b * gain[:, split:]
    u_a, u_b = unit[:, :split], unit[:, split:]
    mean = (
        jnp.sum(g_a * u_a, axis=-1, keepdims=True) + jnp.sum(g_b * u_b, axis=-1, keepdims=True)
    ) / unit.shape[1]
    scale = inv[:, :1]
    out[:, :split] = (cot[:, :split].astype(f32) + scale * (g_a - u_a * mean)).astype(bf16)
    out[:, split:] = (cot[:, split:].astype(f32) + scale * (g_b - u_b * mean)).astype(bf16)


def on_device(
    local_codes,
    local_scales,
    parked_codes,
    parked_scales,
    keep_count,
    roster,
    norm_gain,
    w_gate,
    w_up,
    w_down,
    pending,
):
    sections = lax.axis_size("section")
    _, _, shard, d = local_codes.shape
    stash_pairs = [(sections - 1 - i, i) for i in range(sections // 2)]
    shift_pairs = [((i + 1) % sections, i) for i in range(sections)]

    payload, own_stash, gain, cot_source = local_kernel(
        "prepare",
        prepare_kernel,
        (like(shard, d + EXTRA), like(shard, d + EXTRA + 128), like(1, d, dtype=f32), like(shard, d)),
        keep_count,
        roster,
        parked_codes[0],
        parked_scales[0],
        local_codes[0],
        local_scales[0],
        norm_gain,
        pending[0],
        hbm=True,
        scratch=[
            pltpu.VMEM((2, 2, shard, d), bf16),
            pltpu.VMEM((2, 2, shard), bf16),
            pltpu.SMEM(keep_count.shape, jnp.int32),
            pltpu.SMEM(roster.shape, jnp.int32),
            pltpu.SemaphoreType.DMA((8,)),
        ],
    )
    with jax.named_scope("fetched"):
        fetched = lax.ppermute(payload, "section", stash_pairs)
    with jax.named_scope("shift"):
        cot = lax.ppermute(cot_source, "section", shift_pairs)
    w_gate, w_up, w_down = w_gate[0], w_up[0], w_down[0]
    weights = w_gate, w_up, w_down
    cot = join("cot", cot, after=(own_stash,))
    cot_z = over_tensor("cot_z", cot, other_z)
    cot_core = over_tensor("cot_core", cot, other_core)
    cot_chip = join("cot_chip", cot, cot_core)
    cot_ahead = over_tensor("cot_ahead", cot_chip, along_y)

    normed, unit, inv = local_kernel(
        "norm",
        norm_kernel,
        (like(shard, d), like(shard, d, dtype=f32), like(shard, 128, dtype=f32)),
        own_stash,
        fetched,
        gain,
        after=(cot_chip,),
        flops=LONG,
    )
    normed_z = over_tensor("normed_z", normed, other_z)
    normed_core = over_tensor("normed_core", normed, other_core)
    chip = join("chip", normed, normed_core, after=(cot_z,))
    ahead = over_tensor("ahead", chip, along_y)
    cot_part = join("cot_part", (cot_ahead, 0, 32), after=(normed, chip), columns=d + EXTRA)
    cot_far = over_tensor("cot_far", cot_part, along_y)
    cot_ahead_z = over_tensor("cot_ahead_z", cot_ahead, other_z)
    cot_z_core = over_tensor("cot_z_core", cot_z, other_core)

    normed_z_copies = [
        join(f"normed_z_copy_{at}", (normed_z, at, 16), after=(cot_part,), flops=SHORT) for at in (0, 16)
    ]
    normed_z_core = [over_tensor("normed_z_core", part, other_core) for part in normed_z_copies]
    chip_z = join("chip_z", normed_z, *normed_z_core)
    ahead_z = over_tensor("ahead_z", chip_z, along_y)
    behind = [over_tensor(f"behind_{at}", join(f"behind_{at}", (ahead, at, n)), other_core) for at, n in PARTS]
    cot_behind_z = [
        over_tensor(f"cot_behind_z_{at}", join(f"cot_behind_z_{at}", (cot_ahead_z, at, n)), other_core) for at, n in PARTS
    ]
    cot_far_core = over_tensor("cot_far_core", join("cot_far_part", cot_far, (cot_ahead, 0, 16), columns=d), other_core)
    cot_behind = over_tensor("cot_behind", join("cot_behind_part", (cot_ahead, 16, 48)), other_core)
    cot_far_z = over_tensor("cot_far_z", join("cot_far_copy", cot_far, columns=d), other_z)
    part = join("part", (ahead, 0, 32), (ahead_z, 0, 32))
    far = over_tensor("far", part, along_y)
    behind_z = over_tensor("behind_z", ahead_z, other_core)

    home_blocks = tuple((k, 0, 32) for k in range(4))
    near_blocks = home_blocks + tuple((4 + k, 32 * h, 32) for h in range(2) for k in range(2))
    g1, u1 = hidden(
        "hidden_near",
        (cot, cot_z, cot_core, cot_z_core, cot_ahead, cot_ahead_z),
        near_blocks,
        (normed, normed_z, normed_core, chip_z, ahead, ahead_z),
        tuple((k, 32 if k == 3 else start, n) for k, start, n in near_blocks),
        weights,
        after=(*cot_behind_z, *behind, cot_far_core, cot_behind),
        flops=LONG,
    )
    far_copy = join("far_copy", far, after=(g1,))
    far_core = over_tensor("far_core", far_copy, other_core)
    cot_far_z_copy = join("cot_far_z_copy", cot_far_z, after=(g1,))
    cot_far_z_core = over_tensor("cot_far_z_core", cot_far_z_copy, other_core)
    home_keep, home_send, ahead_keep = back(
        "back_near",
        0,
        d,
        (((0, 64),), ((64, 64),), ((128, 128),)),
        (g1, u1),
        w_gate,
        w_up,
        after=(behind_z, far_copy, cot_far_z_copy),
    )
    home_got = over_tensor("home_got", home_send, other_core)
    g2, u2 = hidden(
        "hidden_rest",
        (cot_far_core, cot_behind, *cot_behind_z, cot_far, cot_far_z, cot_far_z_core),
        ((0, 32, 16), (1, 0, 16), (2, 0, 32), (1, 16, 32), (2, 32, 16), (3, 0, 16),
         (4, 0, 32), (5, 0, 32), (0, 0, 32), (6, 0, 32)),
        (*behind, behind_z, far, far_core),
        ((0, 0, 32), (2, 0, 32), (0, 32, 16), (1, 0, 16), (2, 32, 32), (3, 0, 64), (4, 0, 64)),
        weights,
        after=(home_send,),
        flops=LONG,
    )
    split = Y_FIRST
    rest = ((0, 128), (192, 64)), ((128, 64),)
    send_a, far_a = back("back_a", 0, split, rest, (g2, u2), w_gate, w_up, after=(home_got,), flops=LONG)
    got_a = over_tensor("got_a", send_a, other_core)
    send_b, far_b = back("back_b", split, d - split, rest, (g2, u2), w_gate, w_up, after=(far_a,), flops=LONG)
    got_b = over_tensor("got_b", send_b, other_core)

    to_far = add("to_far", split, [[(64, ((0, 0), (1, 128)))]], far_a, got_a, after=(far_b,))
    from_far = over_tensor("from_far", to_far, back_y)
    to_home_x = add("to_home_x", split, [[(64, ((0, 64), (1, 64)))]], ahead_keep, got_a, after=(to_far,))
    home_x = over_tensor("home_x", to_home_x, back_y)
    pieces_b = (home_keep, split), (home_got, split), (ahead_keep, split), got_b, far_b

    def terms_b(z):
        at = 32 * z
        return ((0, at), (1, at)), ((2, at), (3, at)), ((2, 64 + at), (3, 64 + at)), ((4, at), (3, 128 + at))

    away = add("away", d - split, [[(32, t) for t in terms_b(1)]], *pieces_b, after=(to_home_x,))
    from_z = over_tensor("from_z", away, other_z)
    near = add("near", split, [[(64, ((0, 0), (1, 0)))]], home_keep, home_got, after=(away,))
    to_home = add("to_home", split, [[(64, ((0, 0), (1, 0), (2, 0)))]], ahead_keep, got_a, from_far, after=(near,))
    home = over_tensor("home", to_home, back_y)
    home_x_core = tuple(
        over_tensor(name, join(name + "_part", (home_x, at, 32), after=(to_home,)), other_core)
        for name, at in (("home_x_core", 0), ("home_x_core_z", 32))
    )
    home_own = join("home_own", home_x, after=(to_home,))
    held, held_side, held_far = add(
        "held",
        d - split,
        [[(32, terms_b(0)[k] + ((5, 32 * k),)) for k in ks] for ks in ((0,), (1, 2), (3,))],
        *pieces_b,
        from_z,
        after=(home_own,),
    )
    home_b = over_tensor("home_b", held_side, back_y)
    home_far = over_tensor("home_far", held_far, across_y)
    total, total_away = add(
        "total",
        split,
        [[(32, ((0, at), (1, at), (2 + at // 32, 0)))] for at in (0, 32)],
        near,
        home,
        *home_x_core,
        after=(held,),
    )
    total_z = over_tensor("total_z", total_away, other_z)
    home_b_core = over_tensor("home_b_core", join("home_b_part", (home_b, 32, 32), after=(total, home_far)), other_core)
    return local_kernel(
        "final", final_kernel, like(shard, d), held, home_far, home_b, home_b_core, total, total_z, cot, unit, inv, gain
    )[None]


def solution(mesh):
    placed = (
        P("section", None, "tensor", None),
        P("section", None, "tensor"),
        P("section", None, "tensor", None),
        P("section", None, "tensor"),
        P(),
        P(),
        P("section", None),
        P("section", None, "tensor"),
        P("section", None, "tensor"),
        P("section", "tensor", None),
        P("section", "tensor", None),
    )
    return jax.shard_map(
        on_device,
        mesh=mesh,
        in_specs=placed,
        out_specs=P("section", "tensor", None),
        check_vma=False,
    )
```

```python
import functools

import jax
import jax.numpy as jnp
from jax import lax
from jax.experimental import pallas as pl
from jax.experimental.pallas import tpu as pltpu
from jax.sharding import PartitionSpec as P

bf16 = jnp.bfloat16
f32 = jnp.float32
VMEM = pl.BlockSpec(memory_space=pltpu.VMEM)
MIB = 1024 * 1024
LONG = 10**11
Y_FIRST = 2688
PARTS = (0, 48), (48, 16)
EXTRA = 128
SHORT = 4 * 10**9
HIDDEN_LIMIT = 8
BACK_LIMIT = 8


def like(*shape, dtype=bf16):
    return jax.ShapeDtypeStruct(shape, dtype)


def local_kernel(name, body, outs, *operands, after=(), hbm=False, limit=12, scratch=(), flops=1):
    n_in, n_after = len(operands), len(after)
    anywhere = pl.BlockSpec(memory_space=pl.ANY)
    if hbm:
        operands = tuple(pltpu.with_memory_space_constraint(o, pltpu.HBM) for o in operands)

    def run(*refs):
        body(*refs[:n_in], *refs[n_in + n_after :])

    return pl.pallas_call(
        run,
        out_shape=outs,
        in_specs=[anywhere if hbm else VMEM] * n_in + [anywhere] * n_after,
        out_specs=jax.tree.map(lambda _: VMEM, outs),
        scratch_shapes=scratch,
        compiler_params=pltpu.CompilerParams(vmem_limit_bytes=limit * MIB),
        cost_estimate=pl.CostEstimate(flops=flops, bytes_accessed=1, transcendentals=0),
        name=name,
    )(*operands, *after)


def over_tensor(name, shard, move):
    with jax.named_scope(name):
        return lax.ppermute(shard, "tensor", [(i, move(i)) for i in range(lax.axis_size("tensor"))])


def other_core(i):
    return i ^ 1


def other_z(i):
    return i ^ 2


def along_y(i, sign=1):
    step = sign * (1 if i % 2 == 0 else -1)
    return (i // 4 + step) % 4 * 4 + i % 4


def back_y(i):
    return along_y(i, -1)


def across_y(i):
    return (i + 8) % 16


def join(name, *pieces, after=(), columns=None, flops=1):
    pieces = [p if isinstance(p, tuple) else (p, 0, p.shape[0]) for p in pieces]
    columns = columns or pieces[0][0].shape[1]

    def body(*refs):
        out, at = refs[-1], 0
        for ref, (_, start, n) in zip(refs[:-1], pieces):
            have = min(columns, ref.shape[1])
            out[at : at + n, :have] = ref[start : start + n, :have]
            if have < columns:
                out[at : at + n, have:] = ref[start : start + n, : columns - have]
            at += n

    rows = sum(n for _, _, n in pieces)
    return local_kernel(name, body, like(rows, columns), *[p for p, _, _ in pieces], after=after, flops=flops)


def prepare_kernel(keep_hbm, roster_hbm, parked, parked_scale, local, local_scale, gain, pending,
                   payload, own, gain_copy, cot, codes, scales, keep, roster, sems):
    mine = lax.axis_index("section")
    mirror = lax.axis_size("section") - 1 - mine
    d = gain.shape[1]
    copies = [
        pltpu.make_async_copy(source, target, sems.at[k])
        for k, (source, target) in enumerate(
            (
                (parked, codes.at[0]),
                (parked_scale, scales.at[0]),
                (local, codes.at[1]),
                (local_scale, scales.at[1]),
                (gain, gain_copy),
                (pending, cot),
                (keep_hbm, keep),
                (roster_hbm, roster),
            )
        )
    ]
    for copy in copies:
        copy.start()

    def put(out, which, slot):
        rows = codes.shape[2]
        eye = lax.broadcasted_iota(jnp.int32, (rows, rows), 0) == lax.broadcasted_iota(jnp.int32, (rows, rows), 1)

        def choose(k):
            out[:, :d] = codes[which, k]
            row = jnp.broadcast_to(scales[which, k : k + 1, :].astype(f32), (rows, rows))
            column = jnp.sum(jnp.where(eye, row, 0.0), axis=1, keepdims=True)
            out[:, d : d + EXTRA] = jnp.broadcast_to(column, (rows, EXTRA)).astype(bf16)

        pl.when(slot <= 0)(lambda: choose(0))
        pl.when(slot > 0)(lambda: choose(1))

    for k in (6, 7, 0, 1):
        copies[k].wait()
    put(payload, 0, roster[mirror] - keep[mirror])
    copies[2].wait()
    copies[3].wait()
    put(own, 1, roster[mine])
    is_parked = (roster[mine] >= keep[mine]).astype(f32)
    own[:, d + EXTRA :] = jnp.full((own.shape[0], 128), is_parked, f32).astype(bf16)
    copies[4].wait()
    copies[5].wait()


def norm_kernel(own, parked, gain, normed, unit, inv):
    d = gain.shape[1]
    is_parked = own[:, d + EXTRA : d + EXTRA + 1] > 0
    codes = jnp.where(is_parked, parked[:, :d], own[:, :d])
    scale = jnp.where(is_parked, parked[:, d : d + 1], own[:, d : d + 1])
    x = codes.astype(f32) * scale.astype(f32)
    inv_rms = lax.rsqrt(jnp.mean(x * x, axis=-1, keepdims=True) + 1e-05)
    u = x * inv_rms
    unit[...] = u
    inv[...] = jnp.broadcast_to(inv_rms, inv.shape)
    normed[...] = (u * gain[...]).astype(bf16)


def hidden_kernel(cot_blocks, normed_blocks, n_cot, n_normed, *refs):
    cots, normeds = refs[:n_cot], refs[n_cot : n_cot + n_normed]
    w_gate, w_up, w_down, dgate, dup, rows, dh = refs[n_cot + n_normed :]

    def fill(pieces, blocks):
        at = 0
        for piece, start, count in blocks:
            rows[at : at + count] = pieces[piece][start : start + count, : rows.shape[1]]
            at += count

    fill(cots, cot_blocks)
    dh[...] = lax.dot_general(rows[...], w_down[...], (((1,), (1,)), ((), ())), preferred_element_type=f32)
    fill(normeds, normed_blocks)
    gate = jnp.dot(rows[...], w_gate[...], preferred_element_type=f32)
    up = jnp.dot(rows[...], w_up[...], preferred_element_type=f32)
    d = dh[...]
    sig = jax.nn.sigmoid(gate)
    dgate[...] = (d * up * sig * (1.0 + gate * (1.0 - sig))).astype(bf16)
    dup[...] = (d * gate * sig).astype(bf16)


def hidden(name, cots, cot_blocks, normeds, normed_blocks, weights, after=(), flops=1):
    n_rows = sum(count for _, _, count in cot_blocks)
    d, units = weights[0].shape
    return local_kernel(
        name,
        functools.partial(hidden_kernel, cot_blocks, normed_blocks, len(cots), len(normeds)),
        (like(n_rows, units), like(n_rows, units)),
        *cots,
        *normeds,
        *weights,
        after=after,
        scratch=[pltpu.VMEM((n_rows, d), bf16), pltpu.VMEM((n_rows, units), f32)],
        flops=flops,
        limit=HIDDEN_LIMIT,
    )


def back(name, start, n, outs, grads, w_gate, w_up, after=(), flops=1):
    rows, units = sum(g.shape[0] for g, _ in grads), w_gate.shape[1]

    def body(*refs):
        pairs, (w_gate, w_up), results, all_rows = (
            refs[: 2 * len(grads)],
            refs[2 * len(grads) : 2 * len(grads) + 2],
            refs[2 * len(grads) + 2 : -2],
            refs[-2:],
        )
        at = 0
        for k in range(len(grads)):
            for ref, whole in zip(pairs[2 * k : 2 * k + 2], all_rows):
                whole[at : at + ref.shape[0]] = ref[...]
            at += pairs[2 * k].shape[0]
        g, u = all_rows
        cols = slice(start, start + n)
        transposed = (((1,), (1,)), ((), ()))
        dn = lax.dot_general(g[...], w_gate[cols, :], transposed, preferred_element_type=f32) + lax.dot_general(
            u[...], w_up[cols, :], transposed, preferred_element_type=f32
        )
        for result, spans in zip(results, outs):
            at = 0
            for first, count in spans:
                result[at : at + count] = dn[first : first + count].astype(bf16)
                at += count

    shapes = tuple(like(sum(count for _, count in spans), n) for spans in outs)
    return local_kernel(
        name,
        body,
        shapes,
        *[x for pair in grads for x in pair],
        w_gate,
        w_up,
        after=after,
        scratch=[pltpu.VMEM((rows, units), bf16)] * 2,
        flops=flops,
        limit=BACK_LIMIT,
    )


def add(name, width, outs, *pieces, after=()):
    pieces = [p if isinstance(p, tuple) else (p, 0) for p in pieces]

    def body(*refs):
        for out, spans in zip(refs[len(pieces) :], outs):
            at = 0
            for count, terms in spans:
                total = None
                for piece, start in terms:
                    left = pieces[piece][1]
                    term = refs[piece][start : start + count, left : left + width].astype(f32)
                    total = term if total is None else total + term
                out[at : at + count] = total.astype(out.dtype)
                at += count

    shapes = tuple(like(sum(count for count, _ in spans), width) for spans in outs)
    results = local_kernel(name, body, shapes, *[p for p, _ in pieces], after=after)
    return results if len(outs) > 1 else results[0]


def final_kernel(held, home_far, home_b, other_b, total, total_z, cot, unit, inv, gain, out):
    split = total.shape[1]
    dn_a = total[...].astype(f32) + total_z[...].astype(f32)
    dn_b = held[...].astype(f32) + home_far[...].astype(f32) + home_b[:32].astype(f32) + other_b[...].astype(f32)
    g_a, g_b = dn_a * gain[:, :split], dn_b * gain[:, split:]
    u_a, u_b = unit[:, :split], unit[:, split:]
    mean = (
        jnp.sum(g_a * u_a, axis=-1, keepdims=True) + jnp.sum(g_b * u_b, axis=-1, keepdims=True)
    ) / unit.shape[1]
    scale = inv[:, :1]
    out[:, :split] = (cot[:, :split].astype(f32) + scale * (g_a - u_a * mean)).astype(bf16)
    out[:, split:] = (cot[:, split:].astype(f32) + scale * (g_b - u_b * mean)).astype(bf16)


def on_device(
    local_codes,
    local_scales,
    parked_codes,
    parked_scales,
    keep_count,
    roster,
    norm_gain,
    w_gate,
    w_up,
    w_down,
    pending,
):
    sections = lax.axis_size("section")
    _, _, shard, d = local_codes.shape
    stash_pairs = [(sections - 1 - i, i) for i in range(sections // 2)]
    shift_pairs = [((i + 1) % sections, i) for i in range(sections)]

    payload, own_stash, gain, cot_source = local_kernel(
        "prepare",
        prepare_kernel,
        (like(shard, d + EXTRA), like(shard, d + EXTRA + 128), like(1, d, dtype=f32), like(shard, d)),
        keep_count,
        roster,
        parked_codes[0],
        parked_scales[0],
        local_codes[0],
        local_scales[0],
        norm_gain,
        pending[0],
        hbm=True,
        scratch=[
            pltpu.VMEM((2, 2, shard, d), bf16),
            pltpu.VMEM((2, 2, shard), bf16),
            pltpu.SMEM(keep_count.shape, jnp.int32),
            pltpu.SMEM(roster.shape, jnp.int32),
            pltpu.SemaphoreType.DMA((8,)),
        ],
    )
    with jax.named_scope("fetched"):
        fetched = lax.ppermute(payload, "section", stash_pairs)
    with jax.named_scope("shift"):
        cot = lax.ppermute(cot_source, "section", shift_pairs)
    w_gate, w_up, w_down = w_gate[0], w_up[0], w_down[0]
    weights = w_gate, w_up, w_down
    cot = join("cot", cot, after=(own_stash,))
    cot_z = over_tensor("cot_z", cot, other_z)
    cot_far = over_tensor("cot_far", cot, across_y)
    cot_core = over_tensor("cot_core", cot, other_core)
    cot_chip = join("cot_chip", cot, cot_core)
    cot_ahead = over_tensor("cot_ahead", cot_chip, along_y)

    normed, unit, inv = local_kernel(
        "norm",
        norm_kernel,
        (like(shard, d), like(shard, d, dtype=f32), like(shard, 128, dtype=f32)),
        own_stash,
        fetched,
        gain,
        after=(cot_chip,),
        flops=LONG,
    )
    normed_z = over_tensor("normed_z", normed, other_z)
    normed_core = over_tensor("normed_core", normed, other_core)
    chip = join("chip", normed, normed_core, after=(cot_z, cot_far))
    ahead = over_tensor("ahead", chip, along_y)
    cot_ahead_copy = join("cot_ahead_copy", cot_ahead, after=(normed, chip))
    cot_ahead_z = over_tensor("cot_ahead_z", cot_ahead_copy, other_z)
    cot_behind = over_tensor("cot_behind", cot_ahead, other_core)
    cot_z_core = over_tensor("cot_z_core", cot_z, other_core)

    normed_z_copy = join("normed_z_copy", normed_z, after=(cot_ahead_copy,), flops=SHORT)
    normed_z_core = over_tensor("normed_z_core", normed_z_copy, other_core)
    chip_z = join("chip_z", normed_z, normed_z_core)
    ahead_z = over_tensor("ahead_z", chip_z, along_y)
    cot_far_core = over_tensor("cot_far_core", cot_far, other_core)
    behind = [over_tensor(f"behind_{at}", join(f"behind_{at}", (ahead, at, 32)), other_core) for at in (0, 32)]

    g1, u1 = hidden(
        "hidden_near",
        (cot, cot_z, cot_core, cot_z_core, cot_ahead, cot_behind),
        ((0, 0, 32), (1, 0, 32), (2, 0, 32), (3, 0, 32), (4, 0, 64), (5, 0, 64)),
        (normed, normed_z, normed_core, chip_z, ahead, *behind),
        ((0, 0, 32), (1, 0, 32), (2, 0, 32), (3, 32, 32), (4, 0, 64), (5, 0, 32), (6, 0, 32)),
        weights,
        after=(cot_far_core,),
    )
    cot_behind_z = [
        over_tensor(f"cot_behind_z_{at}", join(f"cot_behind_z_{at}", (cot_ahead_z, at, n), after=(g1,)), other_core)
        for at, n in PARTS
    ]
    cot_far_z = over_tensor("cot_far_z", cot_far, other_z)
    part = join("part", (ahead, 0, 32), (ahead_z, 0, 32), after=(g1,))
    far = over_tensor("far", part, along_y)
    behind_z = over_tensor("behind_z", ahead_z, other_core)
    home_keep, side_keep, near_send = back(
        "back_near",
        0,
        d,
        (((0, 64),), ((128, 64),), ((64, 64), (192, 64))),
        ((g1, u1),),
        w_gate,
        w_up,
        after=(part, *cot_behind_z),
        flops=LONG,
    )
    near_got = over_tensor("near_got", near_send, other_core)
    g2, u2 = hidden(
        "hidden_side_z",
        (cot_ahead_z, *cot_behind_z),
        ((0, 0, 64), (1, 0, 48), (2, 0, 16)),
        (ahead_z, behind_z),
        ((0, 0, 64), (1, 0, 64)),
        weights,
        after=(near_send,),
    )
    far_copy = join("far_copy", far, cot_far_z, after=(g2,))
    far_core = over_tensor("far_core", far_copy, other_core)
    split = Y_FIRST
    g3, u3 = hidden(
        "hidden_far",
        (cot_far, far_copy, cot_far_core, far_core),
        ((0, 0, 32), (1, 64, 32), (2, 0, 32), (3, 64, 32)),
        (far_copy, far_core),
        ((0, 0, 64), (1, 0, 64)),
        weights,
        flops=LONG,
    )
    grads = (g2, u2), (g3, u3)
    rest = ((0, 64),), ((128, 64),), ((64, 64), (192, 64))
    side_a, far_a, send_a = back("back_a", 0, split, rest, grads, w_gate, w_up, after=(near_got,), flops=LONG)
    got_a = over_tensor("got_a", send_a, other_core)
    side_b, far_b, send_b = back("back_b", split, d - split, rest, grads, w_gate, w_up, after=(far_a,), flops=LONG)
    got_b = over_tensor("got_b", send_b, other_core)

    to_far = add("to_far", split, [[(64, ((0, 0), (1, 64)))]], far_a, got_a, after=(far_b,))
    from_far = over_tensor("from_far", to_far, back_y)
    to_home_x = add(
        "to_home_x", split, [[(32, ((0, 32), (1, 96))), (32, ((2, 32), (3, 32)))]], side_keep, near_got, side_a, got_a, after=(to_far,)
    )
    home_x = over_tensor("home_x", to_home_x, back_y)
    away = add(
        "away",
        d - split,
        [[(32, ((0, 32), (1, 32))), (64, ((2, 0), (3, 0))), (32, ((4, 32), (3, 96)))]],
        (home_keep, split),
        (near_got, split),
        side_b,
        got_b,
        far_b,
        after=(to_home_x,),
    )
    from_z = over_tensor("from_z", away, other_z)
    near = add("near", split, [[(64, ((0, 0), (1, 0)))]], home_keep, near_got, after=(away,))
    to_home = add(
        "to_home",
        split,
        [[(32, ((0, 0), (1, 64), (4, 0))), (32, ((2, 0), (3, 0), (4, 32)))]],
        side_keep,
        near_got,
        side_a,
        got_a,
        from_far,
        after=(near,),
    )
    home = over_tensor("home", to_home, back_y)
    home_x_core = tuple(
        over_tensor(name, join(name + "_part", (home_x, at, 32), after=(to_home,)), other_core)
        for name, at in (("home_x_core", 0), ("home_x_core_z", 32))
    )
    home_own = join("home_own", home_x, after=(to_home,))
    held, held_side, held_far = add(
        "held",
        d - split,
        [
            [(32, ((0, 0), (1, 0), (2, 0)))],
            [(64, ((3, 0), (1, 64), (2, 32)))],
            [(32, ((4, 0), (5, 64), (2, 96)))],
        ],
        (home_keep, split),
        (near_got, split),
        from_z,
        (side_keep, split),
        far_b,
        got_b,
        after=(home_own,),
    )
    home_b = over_tensor("home_b", held_side, back_y)
    home_far = over_tensor("home_far", held_far, across_y)
    total, total_away = add(
        "total",
        split,
        [[(32, ((0, at), (1, at), (2 + at // 32, 0)))] for at in (0, 32)],
        near,
        home,
        *home_x_core,
        after=(held,),
    )
    total_z = over_tensor("total_z", total_away, other_z)
    home_b_core = over_tensor("home_b_core", join("home_b_part", (home_b, 32, 32), after=(total, home_far)), other_core)
    return local_kernel(
        "final", final_kernel, like(shard, d), held, home_far, home_b, home_b_core, total, total_z, cot, unit, inv, gain
    )[None]


def solution(mesh):
    placed = (
        P("section", None, "tensor", None),
        P("section", None, "tensor"),
        P("section", None, "tensor", None),
        P("section", None, "tensor"),
        P(),
        P(),
        P("section", None),
        P("section", None, "tensor"),
        P("section", None, "tensor"),
        P("section", "tensor", None),
        P("section", "tensor", None),
    )
    return jax.shard_map(
        on_device,
        mesh=mesh,
        in_specs=placed,
        out_specs=P("section", "tensor", None),
        check_vma=False,
    )
```

```python
import functools

import jax
import jax.numpy as jnp
from jax import lax
from jax.experimental import pallas as pl
from jax.experimental.pallas import tpu as pltpu
from jax.sharding import PartitionSpec as P

bf16 = jnp.bfloat16
f32 = jnp.float32
VMEM = pl.BlockSpec(memory_space=pltpu.VMEM)
MIB = 1024 * 1024
LONG = 10**11
Y_FIRST = 2688
PARTS = (0, 48), (48, 16)
EXTRA = 128
SHORT = 4 * 10**9
HIDDEN_LIMIT = 8
BACK_LIMIT = 8


def like(*shape, dtype=bf16):
    return jax.ShapeDtypeStruct(shape, dtype)


def local_kernel(name, body, outs, *operands, after=(), hbm=False, limit=12, scratch=(), flops=1):
    n_in, n_after = len(operands), len(after)
    anywhere = pl.BlockSpec(memory_space=pl.ANY)
    if hbm:
        operands = tuple(pltpu.with_memory_space_constraint(o, pltpu.HBM) for o in operands)

    def run(*refs):
        body(*refs[:n_in], *refs[n_in + n_after :])

    return pl.pallas_call(
        run,
        out_shape=outs,
        in_specs=[anywhere if hbm else VMEM] * n_in + [anywhere] * n_after,
        out_specs=jax.tree.map(lambda _: VMEM, outs),
        scratch_shapes=scratch,
        compiler_params=pltpu.CompilerParams(vmem_limit_bytes=limit * MIB),
        cost_estimate=pl.CostEstimate(flops=flops, bytes_accessed=1, transcendentals=0),
        name=name,
    )(*operands, *after)


def over_tensor(name, shard, move):
    with jax.named_scope(name):
        return lax.ppermute(shard, "tensor", [(i, move(i)) for i in range(lax.axis_size("tensor"))])


def other_core(i):
    return i ^ 1


def other_z(i):
    return i ^ 2


def along_y(i, sign=1):
    step = sign * (1 if i % 2 == 0 else -1)
    return (i // 4 + step) % 4 * 4 + i % 4


def back_y(i):
    return along_y(i, -1)


def across_y(i):
    return (i + 8) % 16


def join(name, *pieces, after=(), columns=None, flops=1):
    pieces = [p if isinstance(p, tuple) else (p, 0, p.shape[0]) for p in pieces]
    columns = columns or pieces[0][0].shape[1]

    def body(*refs):
        out, at = refs[-1], 0
        for ref, (_, start, n) in zip(refs[:-1], pieces):
            have = min(columns, ref.shape[1])
            out[at : at + n, :have] = ref[start : start + n, :have]
            if have < columns:
                out[at : at + n, have:] = ref[start : start + n, : columns - have]
            at += n

    rows = sum(n for _, _, n in pieces)
    return local_kernel(name, body, like(rows, columns), *[p for p, _, _ in pieces], after=after, flops=flops)


def prepare_kernel(keep_hbm, roster_hbm, parked, parked_scale, local, local_scale, gain,
                   payload, own, gain_copy, codes, scales, keep, roster, sems):
    mine = lax.axis_index("section")
    mirror = lax.axis_size("section") - 1 - mine
    d = gain.shape[1]
    copies = [
        pltpu.make_async_copy(source, target, sems.at[k])
        for k, (source, target) in enumerate(
            (
                (parked, codes.at[0]),
                (parked_scale, scales.at[0]),
                (local, codes.at[1]),
                (local_scale, scales.at[1]),
                (gain, gain_copy),
                (keep_hbm, keep),
                (roster_hbm, roster),
            )
        )
    ]
    for copy in copies:
        copy.start()

    def put(out, which, slot):
        rows = codes.shape[2]
        eye = lax.broadcasted_iota(jnp.int32, (rows, rows), 0) == lax.broadcasted_iota(jnp.int32, (rows, rows), 1)

        def choose(k):
            out[:, :d] = codes[which, k]
            row = jnp.broadcast_to(scales[which, k : k + 1, :].astype(f32), (rows, rows))
            column = jnp.sum(jnp.where(eye, row, 0.0), axis=1, keepdims=True)
            out[:, d : d + EXTRA] = jnp.broadcast_to(column, (rows, EXTRA)).astype(bf16)

        pl.when(slot <= 0)(lambda: choose(0))
        pl.when(slot > 0)(lambda: choose(1))

    for k in (5, 6, 0, 1):
        copies[k].wait()
    put(payload, 0, roster[mirror] - keep[mirror])
    copies[2].wait()
    copies[3].wait()
    put(own, 1, roster[mine])
    is_parked = (roster[mine] >= keep[mine]).astype(f32)
    own[:, d + EXTRA :] = jnp.full((own.shape[0], 128), is_parked, f32).astype(bf16)
    copies[4].wait()


def norm_kernel(own, parked, gain, normed, unit, inv):
    d = gain.shape[1]
    is_parked = own[:, d + EXTRA : d + EXTRA + 1] > 0
    codes = jnp.where(is_parked, parked[:, :d], own[:, :d])
    scale = jnp.where(is_parked, parked[:, d : d + 1], own[:, d : d + 1])
    x = codes.astype(f32) * scale.astype(f32)
    inv_rms = lax.rsqrt(jnp.mean(x * x, axis=-1, keepdims=True) + 1e-05)
    u = x * inv_rms
    unit[...] = u
    inv[...] = jnp.broadcast_to(inv_rms, inv.shape)
    normed[...] = (u * gain[...]).astype(bf16)


def hidden_kernel(cot_blocks, normed_blocks, n_cot, n_normed, *refs):
    cots, normeds = refs[:n_cot], refs[n_cot : n_cot + n_normed]
    w_gate, w_up, w_down, dgate, dup, rows, dh = refs[n_cot + n_normed :]

    def fill(pieces, blocks):
        at = 0
        for piece, start, count in blocks:
            rows[at : at + count] = pieces[piece][start : start + count, : rows.shape[1]]
            at += count

    fill(cots, cot_blocks)
    dh[...] = lax.dot_general(rows[...], w_down[...], (((1,), (1,)), ((), ())), preferred_element_type=f32)
    fill(normeds, normed_blocks)
    gate = jnp.dot(rows[...], w_gate[...], preferred_element_type=f32)
    up = jnp.dot(rows[...], w_up[...], preferred_element_type=f32)
    d = dh[...]
    sig = jax.nn.sigmoid(gate)
    dgate[...] = (d * up * sig * (1.0 + gate * (1.0 - sig))).astype(bf16)
    dup[...] = (d * gate * sig).astype(bf16)


def hidden(name, cots, cot_blocks, normeds, normed_blocks, weights, after=(), flops=1):
    n_rows = sum(count for _, _, count in cot_blocks)
    d, units = weights[0].shape
    return local_kernel(
        name,
        functools.partial(hidden_kernel, cot_blocks, normed_blocks, len(cots), len(normeds)),
        (like(n_rows, units), like(n_rows, units)),
        *cots,
        *normeds,
        *weights,
        after=after,
        scratch=[pltpu.VMEM((n_rows, d), bf16), pltpu.VMEM((n_rows, units), f32)],
        flops=flops,
        limit=HIDDEN_LIMIT,
    )


def back(name, start, n, outs, grads, w_gate, w_up, after=(), flops=1):
    rows, units = sum(g.shape[0] for g, _ in grads), w_gate.shape[1]

    def body(*refs):
        pairs, (w_gate, w_up), results, all_rows = (
            refs[: 2 * len(grads)],
            refs[2 * len(grads) : 2 * len(grads) + 2],
            refs[2 * len(grads) + 2 : -2],
            refs[-2:],
        )
        at = 0
        for k in range(len(grads)):
            for ref, whole in zip(pairs[2 * k : 2 * k + 2], all_rows):
                whole[at : at + ref.shape[0]] = ref[...]
            at += pairs[2 * k].shape[0]
        g, u = all_rows
        cols = slice(start, start + n)
        transposed = (((1,), (1,)), ((), ()))
        dn = lax.dot_general(g[...], w_gate[cols, :], transposed, preferred_element_type=f32) + lax.dot_general(
            u[...], w_up[cols, :], transposed, preferred_element_type=f32
        )
        for result, spans in zip(results, outs):
            at = 0
            for first, count in spans:
                result[at : at + count] = dn[first : first + count].astype(bf16)
                at += count

    shapes = tuple(like(sum(count for _, count in spans), n) for spans in outs)
    return local_kernel(
        name,
        body,
        shapes,
        *[x for pair in grads for x in pair],
        w_gate,
        w_up,
        after=after,
        scratch=[pltpu.VMEM((rows, units), bf16)] * 2,
        flops=flops,
        limit=BACK_LIMIT,
    )


def add(name, width, outs, *pieces, after=()):
    pieces = [p if isinstance(p, tuple) else (p, 0) for p in pieces]

    def body(*refs):
        for out, spans in zip(refs[len(pieces) :], outs):
            at = 0
            for count, terms in spans:
                total = None
                for piece, start in terms:
                    left = pieces[piece][1]
                    term = refs[piece][start : start + count, left : left + width].astype(f32)
                    total = term if total is None else total + term
                out[at : at + count] = total.astype(out.dtype)
                at += count

    shapes = tuple(like(sum(count for count, _ in spans), width) for spans in outs)
    results = local_kernel(name, body, shapes, *[p for p, _ in pieces], after=after)
    return results if len(outs) > 1 else results[0]


def final_kernel(held, home_far, home_b, other_b, total, total_z, cot, unit, inv, gain, out):
    split = total.shape[1]
    dn_a = total[...].astype(f32) + total_z[...].astype(f32)
    dn_b = held[...].astype(f32) + home_far[...].astype(f32) + home_b[:32].astype(f32) + other_b[...].astype(f32)
    g_a, g_b = dn_a * gain[:, :split], dn_b * gain[:, split:]
    u_a, u_b = unit[:, :split], unit[:, split:]
    mean = (
        jnp.sum(g_a * u_a, axis=-1, keepdims=True) + jnp.sum(g_b * u_b, axis=-1, keepdims=True)
    ) / unit.shape[1]
    scale = inv[:, :1]
    out[:, :split] = (cot[:, :split].astype(f32) + scale * (g_a - u_a * mean)).astype(bf16)
    out[:, split:] = (cot[:, split:].astype(f32) + scale * (g_b - u_b * mean)).astype(bf16)


def on_device(
    local_codes,
    local_scales,
    parked_codes,
    parked_scales,
    keep_count,
    roster,
    norm_gain,
    w_gate,
    w_up,
    w_down,
    pending,
):
    sections = lax.axis_size("section")
    _, _, shard, d = local_codes.shape
    stash_pairs = [(sections - 1 - i, i) for i in range(sections // 2)]
    shift_pairs = [((i + 1) % sections, i) for i in range(sections)]

    payload, own_stash, gain = local_kernel(
        "prepare",
        prepare_kernel,
        (like(shard, d + EXTRA), like(shard, d + EXTRA + 128), like(1, d, dtype=f32)),
        keep_count,
        roster,
        parked_codes[0],
        parked_scales[0],
        local_codes[0],
        local_scales[0],
        norm_gain,
        hbm=True,
        scratch=[
            pltpu.VMEM((2, 2, shard, d), bf16),
            pltpu.VMEM((2, 2, shard), bf16),
            pltpu.SMEM(keep_count.shape, jnp.int32),
            pltpu.SMEM(roster.shape, jnp.int32),
            pltpu.SemaphoreType.DMA((7,)),
        ],
    )
    with jax.named_scope("fetched"):
        fetched = lax.ppermute(payload, "section", stash_pairs)
    with jax.named_scope("shift"):
        cot = lax.ppermute(pending[0], "section", shift_pairs)
    w_gate, w_up, w_down = w_gate[0], w_up[0], w_down[0]
    weights = w_gate, w_up, w_down
    cot = join("cot", cot, after=(own_stash,))
    cot_z = over_tensor("cot_z", cot, other_z)
    cot_far = over_tensor("cot_far", cot, across_y)
    cot_core = over_tensor("cot_core", cot, other_core)
    cot_chip = join("cot_chip", cot, cot_core)
    cot_ahead = over_tensor("cot_ahead", cot_chip, along_y)

    normed, unit, inv = local_kernel(
        "norm",
        norm_kernel,
        (like(shard, d), like(shard, d, dtype=f32), like(shard, 128, dtype=f32)),
        own_stash,
        fetched,
        gain,
        after=(cot_chip,),
        flops=LONG,
    )
    normed_z = over_tensor("normed_z", normed, other_z)
    normed_core = over_tensor("normed_core", normed, other_core)
    chip = join("chip", normed, normed_core, after=(cot_z, cot_far))
    ahead = over_tensor("ahead", chip, along_y)
    cot_ahead_copy = join("cot_ahead_copy", cot_ahead, after=(normed, chip))
    cot_ahead_z = over_tensor("cot_ahead_z", cot_ahead_copy, other_z)
    cot_behind = over_tensor("cot_behind", cot_ahead, other_core)
    cot_z_core = over_tensor("cot_z_core", cot_z, other_core)

    normed_z_copy = join("normed_z_copy", normed_z, after=(cot_ahead_copy,), flops=SHORT)
    normed_z_core = over_tensor("normed_z_core", normed_z_copy, other_core)
    chip_z = join("chip_z", normed_z, normed_z_core)
    ahead_z = over_tensor("ahead_z", chip_z, along_y)
    cot_far_core = over_tensor("cot_far_core", cot_far, other_core)
    behind = [over_tensor(f"behind_{at}", join(f"behind_{at}", (ahead, at, 32)), other_core) for at in (0, 32)]

    g1, u1 = hidden(
        "hidden_near",
        (cot, cot_z, cot_core, cot_z_core, cot_ahead, cot_behind),
        ((0, 0, 32), (1, 0, 32), (2, 0, 32), (3, 0, 32), (4, 0, 64), (5, 0, 64)),
        (normed, normed_z, normed_core, chip_z, ahead, *behind),
        ((0, 0, 32), (1, 0, 32), (2, 0, 32), (3, 32, 32), (4, 0, 64), (5, 0, 32), (6, 0, 32)),
        weights,
        after=(cot_far_core,),
    )
    cot_behind_z = [
        over_tensor(f"cot_behind_z_{at}", join(f"cot_behind_z_{at}", (cot_ahead_z, at, n), after=(g1,)), other_core)
        for at, n in PARTS
    ]
    cot_far_z = over_tensor("cot_far_z", cot_far, other_z)
    part = join("part", (ahead, 0, 32), (ahead_z, 0, 32), after=(g1,))
    far = over_tensor("far", part, along_y)
    behind_z = over_tensor("behind_z", ahead_z, other_core)
    home_keep, side_keep, near_send = back(
        "back_near",
        0,
        d,
        (((0, 64),), ((128, 64),), ((64, 64), (192, 64))),
        ((g1, u1),),
        w_gate,
        w_up,
        after=(part, *cot_behind_z),
        flops=LONG,
    )
    near_got = over_tensor("near_got", near_send, other_core)
    g2, u2 = hidden(
        "hidden_side_z",
        (cot_ahead_z, *cot_behind_z),
        ((0, 0, 64), (1, 0, 48), (2, 0, 16)),
        (ahead_z, behind_z),
        ((0, 0, 64), (1, 0, 64)),
        weights,
        after=(near_send,),
    )
    far_copy = join("far_copy", far, cot_far_z, after=(g2,))
    far_core = over_tensor("far_core", far_copy, other_core)
    split = Y_FIRST
    g3, u3 = hidden(
        "hidden_far",
        (cot_far, far_copy, cot_far_core, far_core),
        ((0, 0, 32), (1, 64, 32), (2, 0, 32), (3, 64, 32)),
        (far_copy, far_core),
        ((0, 0, 64), (1, 0, 64)),
        weights,
        flops=LONG,
    )
    grads = (g2, u2), (g3, u3)
    rest = ((0, 64),), ((128, 64),), ((64, 64), (192, 64))
    side_a, far_a, send_a = back("back_a", 0, split, rest, grads, w_gate, w_up, after=(near_got,), flops=LONG)
    got_a = over_tensor("got_a", send_a, other_core)
    side_b, far_b, send_b = back("back_b", split, d - split, rest, grads, w_gate, w_up, after=(far_a,), flops=LONG)
    got_b = over_tensor("got_b", send_b, other_core)

    to_far = add("to_far", split, [[(64, ((0, 0), (1, 64)))]], far_a, got_a, after=(far_b,))
    from_far = over_tensor("from_far", to_far, back_y)
    to_home_x = add(
        "to_home_x", split, [[(32, ((0, 32), (1, 96))), (32, ((2, 32), (3, 32)))]], side_keep, near_got, side_a, got_a, after=(to_far,)
    )
    home_x = over_tensor("home_x", to_home_x, back_y)
    away = add(
        "away",
        d - split,
        [[(32, ((0, 32), (1, 32))), (64, ((2, 0), (3, 0))), (32, ((4, 32), (3, 96)))]],
        (home_keep, split),
        (near_got, split),
        side_b,
        got_b,
        far_b,
        after=(to_home_x,),
    )
    from_z = over_tensor("from_z", away, other_z)
    near = add("near", split, [[(64, ((0, 0), (1, 0)))]], home_keep, near_got, after=(away,))
    to_home = add(
        "to_home",
        split,
        [[(32, ((0, 0), (1, 64), (4, 0))), (32, ((2, 0), (3, 0), (4, 32)))]],
        side_keep,
        near_got,
        side_a,
        got_a,
        from_far,
        after=(near,),
    )
    home = over_tensor("home", to_home, back_y)
    home_x_core = tuple(
        over_tensor(name, join(name + "_part", (home_x, at, 32), after=(to_home,)), other_core)
        for name, at in (("home_x_core", 0), ("home_x_core_z", 32))
    )
    home_own = join("home_own", home_x, after=(to_home,))
    held, held_side, held_far = add(
        "held",
        d - split,
        [
            [(32, ((0, 0), (1, 0), (2, 0)))],
            [(64, ((3, 0), (1, 64), (2, 32)))],
            [(32, ((4, 0), (5, 64), (2, 96)))],
        ],
        (home_keep, split),
        (near_got, split),
        from_z,
        (side_keep, split),
        far_b,
        got_b,
        after=(home_own,),
    )
    home_b = over_tensor("home_b", held_side, back_y)
    home_far = over_tensor("home_far", held_far, across_y)
    total, total_away = add(
        "total",
        split,
        [[(32, ((0, at), (1, at), (2 + at // 32, 0)))] for at in (0, 32)],
        near,
        home,
        *home_x_core,
        after=(held,),
    )
    total_z = over_tensor("total_z", total_away, other_z)
    home_b_core = over_tensor("home_b_core", join("home_b_part", (home_b, 32, 32), after=(total, home_far)), other_core)
    return local_kernel(
        "final", final_kernel, like(shard, d), held, home_far, home_b, home_b_core, total, total_z, cot, unit, inv, gain
    )[None]


def solution(mesh):
    placed = (
        P("section", None, "tensor", None),
        P("section", None, "tensor"),
        P("section", None, "tensor", None),
        P("section", None, "tensor"),
        P(),
        P(),
        P("section", None),
        P("section", None, "tensor"),
        P("section", None, "tensor"),
        P("section", "tensor", None),
        P("section", "tensor", None),
    )
    return jax.shard_map(
        on_device,
        mesh=mesh,
        in_specs=placed,
        out_specs=P("section", "tensor", None),
        check_vma=False,
    )
```

```python
import functools

import jax
import jax.numpy as jnp
from jax import lax
from jax.experimental import pallas as pl
from jax.experimental.pallas import tpu as pltpu
from jax.sharding import PartitionSpec as P

bf16 = jnp.bfloat16
f32 = jnp.float32
VMEM = pl.BlockSpec(memory_space=pltpu.VMEM)
MIB = 1024 * 1024
LONG = 10**11
Y_FIRST = 2688
PARTS = (0, 48), (48, 16)
EXTRA = 128
SHORT = 4 * 10**9
HIDDEN_LIMIT = 8
BACK_LIMIT = 8


def like(*shape, dtype=bf16):
    return jax.ShapeDtypeStruct(shape, dtype)


def local_kernel(name, body, outs, *operands, after=(), hbm=False, limit=12, scratch=(), flops=1):
    n_in, n_after = len(operands), len(after)
    anywhere = pl.BlockSpec(memory_space=pl.ANY)
    if hbm:
        operands = tuple(pltpu.with_memory_space_constraint(o, pltpu.HBM) for o in operands)

    def run(*refs):
        body(*refs[:n_in], *refs[n_in + n_after :])

    return pl.pallas_call(
        run,
        out_shape=outs,
        in_specs=[anywhere if hbm else VMEM] * n_in + [anywhere] * n_after,
        out_specs=jax.tree.map(lambda _: VMEM, outs),
        scratch_shapes=scratch,
        compiler_params=pltpu.CompilerParams(vmem_limit_bytes=limit * MIB),
        cost_estimate=pl.CostEstimate(flops=flops, bytes_accessed=1, transcendentals=0),
        name=name,
    )(*operands, *after)


def over_tensor(name, shard, move):
    with jax.named_scope(name):
        return lax.ppermute(shard, "tensor", [(i, move(i)) for i in range(lax.axis_size("tensor"))])


def other_core(i):
    return i ^ 1


def other_z(i):
    return i ^ 2


def along_y(i, sign=1):
    step = sign * (1 if i % 2 == 0 else -1)
    return (i // 4 + step) % 4 * 4 + i % 4


def back_y(i):
    return along_y(i, -1)


def across_y(i):
    return (i + 8) % 16


def join(name, *pieces, after=(), columns=None, flops=1):
    pieces = [p if isinstance(p, tuple) else (p, 0, p.shape[0]) for p in pieces]
    columns = columns or pieces[0][0].shape[1]

    def body(*refs):
        out, at = refs[-1], 0
        for ref, (_, start, n) in zip(refs[:-1], pieces):
            have = min(columns, ref.shape[1])
            out[at : at + n, :have] = ref[start : start + n, :have]
            if have < columns:
                out[at : at + n, have:] = ref[start : start + n, : columns - have]
            at += n

    rows = sum(n for _, _, n in pieces)
    return local_kernel(name, body, like(rows, columns), *[p for p, _, _ in pieces], after=after, flops=flops)


def prepare_kernel(keep_hbm, roster_hbm, parked, parked_scale, local, local_scale, gain,
                   payload, own, gain_copy, codes, scales, keep, roster, sems):
    mine = lax.axis_index("section")
    mirror = lax.axis_size("section") - 1 - mine
    d = gain.shape[1]
    copies = [
        pltpu.make_async_copy(source, target, sems.at[k])
        for k, (source, target) in enumerate(
            (
                (parked, codes.at[0]),
                (parked_scale, scales.at[0]),
                (local, codes.at[1]),
                (local_scale, scales.at[1]),
                (gain, gain_copy),
                (keep_hbm, keep),
                (roster_hbm, roster),
            )
        )
    ]
    for copy in copies:
        copy.start()

    def put(out, which, slot):
        rows = codes.shape[2]
        eye = lax.broadcasted_iota(jnp.int32, (rows, rows), 0) == lax.broadcasted_iota(jnp.int32, (rows, rows), 1)

        def choose(k):
            out[:, :d] = codes[which, k]
            row = jnp.broadcast_to(scales[which, k : k + 1, :].astype(f32), (rows, rows))
            column = jnp.sum(jnp.where(eye, row, 0.0), axis=1, keepdims=True)
            out[:, d : d + EXTRA] = jnp.broadcast_to(column, (rows, EXTRA)).astype(bf16)

        pl.when(slot <= 0)(lambda: choose(0))
        pl.when(slot > 0)(lambda: choose(1))

    for k in (5, 6, 0, 1):
        copies[k].wait()
    put(payload, 0, roster[mirror] - keep[mirror])
    copies[2].wait()
    copies[3].wait()
    put(own, 1, roster[mine])
    is_parked = (roster[mine] >= keep[mine]).astype(f32)
    own[:, d + EXTRA :] = jnp.full((own.shape[0], 128), is_parked, f32).astype(bf16)
    copies[4].wait()


def norm_kernel(own, parked, gain, normed, unit, inv):
    d = gain.shape[1]
    is_parked = own[:, d + EXTRA : d + EXTRA + 1] > 0
    codes = jnp.where(is_parked, parked[:, :d], own[:, :d])
    scale = jnp.where(is_parked, parked[:, d : d + 1], own[:, d : d + 1])
    x = codes.astype(f32) * scale.astype(f32)
    inv_rms = lax.rsqrt(jnp.mean(x * x, axis=-1, keepdims=True) + 1e-05)
    u = x * inv_rms
    unit[...] = u
    inv[...] = jnp.broadcast_to(inv_rms, inv.shape)
    normed[...] = (u * gain[...]).astype(bf16)


def hidden_kernel(cot_blocks, normed_blocks, n_cot, n_normed, *refs):
    cots, normeds = refs[:n_cot], refs[n_cot : n_cot + n_normed]
    w_gate, w_up, w_down, dgate, dup, rows, dh = refs[n_cot + n_normed :]

    def fill(pieces, blocks):
        at = 0
        for piece, start, count in blocks:
            rows[at : at + count] = pieces[piece][start : start + count, : rows.shape[1]]
            at += count

    fill(cots, cot_blocks)
    dh[...] = lax.dot_general(rows[...], w_down[...], (((1,), (1,)), ((), ())), preferred_element_type=f32)
    fill(normeds, normed_blocks)
    gate = jnp.dot(rows[...], w_gate[...], preferred_element_type=f32)
    up = jnp.dot(rows[...], w_up[...], preferred_element_type=f32)
    d = dh[...]
    sig = jax.nn.sigmoid(gate)
    dgate[...] = (d * up * sig * (1.0 + gate * (1.0 - sig))).astype(bf16)
    dup[...] = (d * gate * sig).astype(bf16)


def hidden(name, cots, cot_blocks, normeds, normed_blocks, weights, after=(), flops=1):
    n_rows = sum(count for _, _, count in cot_blocks)
    d, units = weights[0].shape
    return local_kernel(
        name,
        functools.partial(hidden_kernel, cot_blocks, normed_blocks, len(cots), len(normeds)),
        (like(n_rows, units), like(n_rows, units)),
        *cots,
        *normeds,
        *weights,
        after=after,
        scratch=[pltpu.VMEM((n_rows, d), bf16), pltpu.VMEM((n_rows, units), f32)],
        flops=flops,
        limit=HIDDEN_LIMIT,
    )


def back(name, start, n, outs, grads, w_gate, w_up, after=(), flops=1):
    rows, units = sum(g.shape[0] for g, _ in grads), w_gate.shape[1]

    def body(*refs):
        pairs, (w_gate, w_up), results, all_rows = (
            refs[: 2 * len(grads)],
            refs[2 * len(grads) : 2 * len(grads) + 2],
            refs[2 * len(grads) + 2 : -2],
            refs[-2:],
        )
        at = 0
        for k in range(len(grads)):
            for ref, whole in zip(pairs[2 * k : 2 * k + 2], all_rows):
                whole[at : at + ref.shape[0]] = ref[...]
            at += pairs[2 * k].shape[0]
        g, u = all_rows
        cols = slice(start, start + n)
        transposed = (((1,), (1,)), ((), ()))
        dn = lax.dot_general(g[...], w_gate[cols, :], transposed, preferred_element_type=f32) + lax.dot_general(
            u[...], w_up[cols, :], transposed, preferred_element_type=f32
        )
        for result, spans in zip(results, outs):
            at = 0
            for first, count in spans:
                result[at : at + count] = dn[first : first + count].astype(bf16)
                at += count

    shapes = tuple(like(sum(count for _, count in spans), n) for spans in outs)
    return local_kernel(
        name,
        body,
        shapes,
        *[x for pair in grads for x in pair],
        w_gate,
        w_up,
        after=after,
        scratch=[pltpu.VMEM((rows, units), bf16)] * 2,
        flops=flops,
        limit=BACK_LIMIT,
    )


def add(name, width, outs, *pieces, after=()):
    pieces = [p if isinstance(p, tuple) else (p, 0) for p in pieces]

    def body(*refs):
        for out, spans in zip(refs[len(pieces) :], outs):
            at = 0
            for count, terms in spans:
                total = None
                for piece, start in terms:
                    left = pieces[piece][1]
                    term = refs[piece][start : start + count, left : left + width].astype(f32)
                    total = term if total is None else total + term
                out[at : at + count] = total.astype(out.dtype)
                at += count

    shapes = tuple(like(sum(count for count, _ in spans), width) for spans in outs)
    results = local_kernel(name, body, shapes, *[p for p, _ in pieces], after=after)
    return results if len(outs) > 1 else results[0]


def final_kernel(held, home_far, home_b, other_b, total, total_z, cot, unit, inv, gain, out):
    split = total.shape[1]
    dn_a = total[...].astype(f32) + total_z[...].astype(f32)
    dn_b = held[...].astype(f32) + home_far[...].astype(f32) + home_b[:32].astype(f32) + other_b[...].astype(f32)
    g_a, g_b = dn_a * gain[:, :split], dn_b * gain[:, split:]
    u_a, u_b = unit[:, :split], unit[:, split:]
    mean = (
        jnp.sum(g_a * u_a, axis=-1, keepdims=True) + jnp.sum(g_b * u_b, axis=-1, keepdims=True)
    ) / unit.shape[1]
    scale = inv[:, :1]
    out[:, :split] = (cot[:, :split].astype(f32) + scale * (g_a - u_a * mean)).astype(bf16)
    out[:, split:] = (cot[:, split:].astype(f32) + scale * (g_b - u_b * mean)).astype(bf16)


def on_device(
    local_codes,
    local_scales,
    parked_codes,
    parked_scales,
    keep_count,
    roster,
    norm_gain,
    w_gate,
    w_up,
    w_down,
    pending,
):
    sections = lax.axis_size("section")
    _, _, shard, d = local_codes.shape
    stash_pairs = [(sections - 1 - i, i) for i in range(sections // 2)]
    shift_pairs = [((i + 1) % sections, i) for i in range(sections)]

    payload, own_stash, gain = local_kernel(
        "prepare",
        prepare_kernel,
        (like(shard, d + EXTRA), like(shard, d + EXTRA + 128), like(1, d, dtype=f32)),
        keep_count,
        roster,
        parked_codes[0],
        parked_scales[0],
        local_codes[0],
        local_scales[0],
        norm_gain,
        hbm=True,
        scratch=[
            pltpu.VMEM((2, 2, shard, d), bf16),
            pltpu.VMEM((2, 2, shard), bf16),
            pltpu.SMEM(keep_count.shape, jnp.int32),
            pltpu.SMEM(roster.shape, jnp.int32),
            pltpu.SemaphoreType.DMA((7,)),
        ],
    )
    with jax.named_scope("fetched"):
        fetched = lax.ppermute(payload, "section", stash_pairs)
    with jax.named_scope("shift"):
        cot = lax.ppermute(pending[0], "section", shift_pairs)
    w_gate, w_up, w_down = w_gate[0], w_up[0], w_down[0]
    weights = w_gate, w_up, w_down
    cot_z = over_tensor("cot_z", cot, other_z)
    cot_far = over_tensor("cot_far", cot, across_y)
    cot_core = over_tensor("cot_core", cot, other_core)
    cot_chip = join("cot_chip", cot, cot_core)
    cot_ahead = over_tensor("cot_ahead", cot_chip, along_y)

    normed, unit, inv = local_kernel(
        "norm",
        norm_kernel,
        (like(shard, d), like(shard, d, dtype=f32), like(shard, 128, dtype=f32)),
        own_stash,
        fetched,
        gain,
        after=(cot_chip,),
        flops=LONG,
    )
    normed_z = over_tensor("normed_z", normed, other_z)
    normed_core = over_tensor("normed_core", normed, other_core)
    chip = join("chip", normed, normed_core, after=(cot_z, cot_far))
    ahead = over_tensor("ahead", chip, along_y)
    cot_ahead_copy = join("cot_ahead_copy", cot_ahead, after=(normed, chip))
    cot_ahead_z = over_tensor("cot_ahead_z", cot_ahead_copy, other_z)
    cot_behind = over_tensor("cot_behind", cot_ahead, other_core)
    cot_z_core = over_tensor("cot_z_core", cot_z, other_core)

    normed_z_copy = join("normed_z_copy", normed_z, after=(cot_ahead_copy,), flops=SHORT)
    normed_z_core = over_tensor("normed_z_core", normed_z_copy, other_core)
    chip_z = join("chip_z", normed_z, normed_z_core)
    ahead_z = over_tensor("ahead_z", chip_z, along_y)
    cot_far_core = over_tensor("cot_far_core", cot_far, other_core)
    behind = [over_tensor(f"behind_{at}", join(f"behind_{at}", (ahead, at, 32)), other_core) for at in (0, 32)]

    g1, u1 = hidden(
        "hidden_near",
        (cot, cot_z, cot_core, cot_z_core, cot_ahead, cot_behind),
        ((0, 0, 32), (1, 0, 32), (2, 0, 32), (3, 0, 32), (4, 0, 64), (5, 0, 64)),
        (normed, normed_z, normed_core, chip_z, ahead, *behind),
        ((0, 0, 32), (1, 0, 32), (2, 0, 32), (3, 32, 32), (4, 0, 64), (5, 0, 32), (6, 0, 32)),
        weights,
        after=(cot_far_core,),
    )
    cot_behind_z = [
        over_tensor(f"cot_behind_z_{at}", join(f"cot_behind_z_{at}", (cot_ahead_z, at, n), after=(g1,)), other_core)
        for at, n in PARTS
    ]
    cot_far_z = over_tensor("cot_far_z", cot_far, other_z)
    part = join("part", (ahead, 0, 32), (ahead_z, 0, 32), after=(g1,))
    far = over_tensor("far", part, along_y)
    behind_z = over_tensor("behind_z", ahead_z, other_core)
    home_keep, side_keep, near_send = back(
        "back_near",
        0,
        d,
        (((0, 64),), ((128, 64),), ((64, 64), (192, 64))),
        ((g1, u1),),
        w_gate,
        w_up,
        after=(part, *cot_behind_z),
        flops=LONG,
    )
    near_got = over_tensor("near_got", near_send, other_core)
    g2, u2 = hidden(
        "hidden_side_z",
        (cot_ahead_z, *cot_behind_z),
        ((0, 0, 64), (1, 0, 48), (2, 0, 16)),
        (ahead_z, behind_z),
        ((0, 0, 64), (1, 0, 64)),
        weights,
        after=(near_send,),
    )
    far_copy = join("far_copy", far, cot_far_z, after=(g2,))
    far_core = over_tensor("far_core", far_copy, other_core)
    split = Y_FIRST
    g3, u3 = hidden(
        "hidden_far",
        (cot_far, far_copy, cot_far_core, far_core),
        ((0, 0, 32), (1, 64, 32), (2, 0, 32), (3, 64, 32)),
        (far_copy, far_core),
        ((0, 0, 64), (1, 0, 64)),
        weights,
        flops=LONG,
    )
    grads = (g2, u2), (g3, u3)
    rest = ((0, 64),), ((128, 64),), ((64, 64), (192, 64))
    side_a, far_a, send_a = back("back_a", 0, split, rest, grads, w_gate, w_up, after=(near_got,), flops=LONG)
    got_a = over_tensor("got_a", send_a, other_core)
    side_b, far_b, send_b = back("back_b", split, d - split, rest, grads, w_gate, w_up, after=(far_a,), flops=LONG)
    got_b = over_tensor("got_b", send_b, other_core)

    to_far = add("to_far", split, [[(64, ((0, 0), (1, 64)))]], far_a, got_a, after=(far_b,))
    from_far = over_tensor("from_far", to_far, back_y)
    to_home_x = add(
        "to_home_x", split, [[(32, ((0, 32), (1, 96))), (32, ((2, 32), (3, 32)))]], side_keep, near_got, side_a, got_a, after=(to_far,)
    )
    home_x = over_tensor("home_x", to_home_x, back_y)
    away = add(
        "away",
        d - split,
        [[(32, ((0, 32), (1, 32))), (64, ((2, 0), (3, 0))), (32, ((4, 32), (3, 96)))]],
        (home_keep, split),
        (near_got, split),
        side_b,
        got_b,
        far_b,
        after=(to_home_x,),
    )
    from_z = over_tensor("from_z", away, other_z)
    near = add("near", split, [[(64, ((0, 0), (1, 0)))]], home_keep, near_got, after=(away,))
    to_home = add(
        "to_home",
        split,
        [[(32, ((0, 0), (1, 64), (4, 0))), (32, ((2, 0), (3, 0), (4, 32)))]],
        side_keep,
        near_got,
        side_a,
        got_a,
        from_far,
        after=(near,),
    )
    home = over_tensor("home", to_home, back_y)
    home_x_core = tuple(
        over_tensor(name, join(name + "_part", (home_x, at, 32), after=(to_home,)), other_core)
        for name, at in (("home_x_core", 0), ("home_x_core_z", 32))
    )
    home_own = join("home_own", home_x, after=(to_home,))
    held, held_side, held_far = add(
        "held",
        d - split,
        [
            [(32, ((0, 0), (1, 0), (2, 0)))],
            [(64, ((3, 0), (1, 64), (2, 32)))],
            [(32, ((4, 0), (5, 64), (2, 96)))],
        ],
        (home_keep, split),
        (near_got, split),
        from_z,
        (side_keep, split),
        far_b,
        got_b,
        after=(home_own,),
    )
    home_b = over_tensor("home_b", held_side, back_y)
    home_far = over_tensor("home_far", held_far, across_y)
    total, total_away = add(
        "total",
        split,
        [[(32, ((0, at), (1, at), (2 + at // 32, 0)))] for at in (0, 32)],
        near,
        home,
        *home_x_core,
        after=(held,),
    )
    total_z = over_tensor("total_z", total_away, other_z)
    home_b_core = over_tensor("home_b_core", join("home_b_part", (home_b, 32, 32), after=(total, home_far)), other_core)
    return local_kernel(
        "final", final_kernel, like(shard, d), held, home_far, home_b, home_b_core, total, total_z, cot, unit, inv, gain
    )[None]


def solution(mesh):
    placed = (
        P("section", None, "tensor", None),
        P("section", None, "tensor"),
        P("section", None, "tensor", None),
        P("section", None, "tensor"),
        P(),
        P(),
        P("section", None),
        P("section", None, "tensor"),
        P("section", None, "tensor"),
        P("section", "tensor", None),
        P("section", "tensor", None),
    )
    return jax.shard_map(
        on_device,
        mesh=mesh,
        in_specs=placed,
        out_specs=P("section", "tensor", None),
        check_vma=False,
    )
```
